32 devices in a mesh: rep: 4 (over y, x), shard: 8 (over z, core).
Axes of the slice: x: 2, y: 2, z: 4, core: 2. Of those that a mesh axis runs over, the one named last changes fastest.
Arguments:
- grad_wide: float32 [4, 1, 384, 5376], P('rep', None, 'shard')
- grad_down: float32 [4, 1, 1536, 384], P('rep', None, None, 'shard')
- grad_embed: float32 [4, 1001, 384], P('rep', None, 'shard')
- mom_wide: float32 [1, 384, 5376], P(None, 'shard'), may hold values from -6 to 6
- mom_down: float32 [1, 1536, 384], P(None, None, 'shard'), may hold values from -6 to 6
- mom_embed: float32 [1001, 384], P(None, 'shard'), may hold values from -6 to 6
Outputs:
- new_mom_wide: float32 [1, 384, 5376], P(None, 'shard')
- new_mom_down: float32 [1, 1536, 384], P(None, None, 'shard')
- new_mom_embed: float32 [1001, 384], P(None, 'shard')
- upd_wide: bfloat16 [1, 384, 5376], P(None, 'shard')
- upd_down: bfloat16 [1, 1536, 384], P(None, None, 'shard')
- upd_embed: bfloat16 [1001, 384], P(None, 'shard')
The draws below stay inside these ranges and needn't reach their ends.
All inputs are finite; a program needn't handle non-finite values.
Results may differ from the reference program's by a relative error of at most 0.03.
Values may be sent and summed in bfloat16 or wider, within the bound.
No kernel may reach another device: no remote copies, remote signals or barrier semaphores. Data moves between devices by JAX's collectives and lax.ppermute only.
A program may use at most 64 MiB of HBM per device.

```python
import math
import jax
import jax.numpy as jnp
from jax import lax

D = 384
MLP = 1536
ADA = 2304
CLASSES = 1001
BLOCKS = 1
NS_ITERS = 5
QKV = 1152
WIDE = 5376
N_REP = 4


def scaled_gradient(key, lead, row_total, column_total):
    key_base, key_rows, key_columns = jax.random.split(key, 3)
    base = jax.random.normal(key_base, lead + (row_total, column_total), jnp.float32)
    row_scale = jnp.exp(jax.random.uniform(key_rows, (row_total, 1), jnp.float32, jnp.log(0.3), jnp.log(3.0)))
    column_scale = jnp.exp(jax.random.uniform(key_columns, (1, column_total), jnp.float32, jnp.log(0.3), jnp.log(3.0)))
    return base * row_scale * column_scale


def draw_grad_wide(key, part):
    return scaled_gradient(jax.random.fold_in(key, 11), (N_REP, BLOCKS), D, WIDE)


def draw_grad_down(key, part):
    return scaled_gradient(jax.random.fold_in(key, 12), (N_REP, BLOCKS), MLP, D)


def draw_grad_embed(key, part):
    return scaled_gradient(jax.random.fold_in(key, 13), (N_REP,), CLASSES, D)


def levels(own_key, dims, cuts, low, largest):
    loudness = 1.0
    for position, parts in cuts:
        heights = jax.random.uniform(jax.random.fold_in(jax.random.fold_in(own_key, 6), position), (parts,), jnp.float32, low / len(cuts), largest / len(cuts))
        loudness = loudness * jnp.repeat(jnp.exp(heights), dims[position] // parts).reshape((-1,) + (1,) * (len(dims) - 1 - position))
    return loudness


def normal_values(stream_key, dims, spread, limit, shards=(), held_as=jnp.bfloat16):
    array = jax.random.normal(stream_key, dims, jnp.float32) * spread
    if len(shards) > 0:
        array = levels(stream_key, dims, shards, -0.22, 0.18) * array
    return jnp.clip(array, min=-limit, max=limit).astype(held_as)


def setup_inputs(seed: int = 0) -> dict:
    key_of = jax.random.split(jax.random.key(seed), 7)
    grad_wide = draw_grad_wide(jax.random.fold_in(key_of[6], 71), 0)
    grad_down = draw_grad_down(jax.random.fold_in(key_of[6], 71), 0)
    grad_embed = draw_grad_embed(jax.random.fold_in(key_of[6], 71), 0)
    mom_wide = normal_values(key_of[3], (BLOCKS, D, WIDE), 1.0, 6.0, ((1, 8),), jnp.float32)
    mom_down = normal_values(key_of[4], (BLOCKS, MLP, D), 1.0, 6.0, ((2, 8),), jnp.float32)
    mom_embed = normal_values(key_of[5], (CLASSES, D), 1.0, 6.0, ((1, 8),), jnp.float32)
    return {"grad_wide": grad_wide, "grad_down": grad_down, "grad_embed": grad_embed, "mom_wide": mom_wide, "mom_down": mom_down, "mom_embed": mom_embed}


COEF_A = 3.4445
COEF_B = -4.775
COEF_C = 2.0315
MOMENTUM = 0.95
EPSILON = 1e-07

def orthogonal_update(nesterov):
    norm_value = jnp.sqrt(jnp.sum(nesterov * nesterov)) + EPSILON
    iterate = (nesterov / norm_value).astype(jnp.bfloat16)
    for sweep in range(NS_ITERS):
        gram = jnp.dot(iterate, iterate.T, preferred_element_type=jnp.float32).astype(jnp.bfloat16)
        polynomial = (COEF_B * gram.astype(jnp.float32) + COEF_C * jnp.dot(gram, gram, preferred_element_type=jnp.float32)).astype(jnp.bfloat16)
        iterate = (COEF_A * iterate.astype(jnp.float32) + jnp.dot(polynomial, iterate, preferred_element_type=jnp.float32)).astype(jnp.bfloat16)
    factor = math.sqrt(max(D, nesterov.shape[1]))
    return (iterate.astype(jnp.float32) * factor).astype(jnp.bfloat16)

def reference(grad_wide, grad_down, grad_embed, mom_wide, mom_down, mom_embed):
    g_wide = lax.optimization_barrier(jnp.sum(grad_wide, axis=0))
    g_down = lax.optimization_barrier(jnp.sum(grad_down, axis=0))
    g_embed = lax.optimization_barrier(jnp.sum(grad_embed, axis=0))
    new_wide = MOMENTUM * mom_wide + g_wide
    new_down = MOMENTUM * mom_down + g_down
    new_embed = MOMENTUM * mom_embed + g_embed
    nest_wide = g_wide + MOMENTUM * new_wide
    nest_down = g_down + MOMENTUM * new_down
    nest_embed = g_embed + MOMENTUM * new_embed
    segments = [(0, QKV), (QKV, D), (QKV + D, MLP), (QKV + D + MLP, ADA)]
    wide_list = []
    down_list = []
    for block in range(BLOCKS):
        pieces = [orthogonal_update(nest_wide[block][:, offset:offset + width]) for offset, width in segments]
        wide_list.append(jnp.concatenate(pieces, axis=1))
        down_list.append(orthogonal_update(nest_down[block].T).T)
    upd_wide = jnp.stack(wide_list)
    upd_down = jnp.stack(down_list)
    upd_embed = orthogonal_update(nest_embed.T).T
    return (new_wide, new_down, new_embed, upd_wide, upd_down, upd_embed)
```

```python
import functools
import math

import jax
import jax.numpy as jnp
from jax import lax
from jax.experimental import pallas as pl
from jax.experimental.pallas import tpu as pltpu
from jax.sharding import PartitionSpec as P

D = 384
MLP = 1536
ADA = 2304
CLASSES = 1001
NS_ITERS = 5
QKV = 1152

COEF_A = 3.4445
COEF_B = -4.775
COEF_C = 2.0315
MOMENTUM = 0.95
EPSILON = 1e-07

VMEM_LIMIT = 48 * 1024 * 1024

WIDTHS = [QKV, D, MLP, ADA, MLP, CLASSES]
OFFSETS = [0, QKV, QKV + D, QKV + D + MLP]
PADDED = [-(-width // 128) * 128 for width in WIDTHS]
DOWN, EMBED = 4, 5


def plan(n_rep):
    bins = [[] for _ in range(n_rep)]
    loads = [0] * n_rep
    for matrix in sorted(range(6), key=lambda m: -PADDED[m]):
        owner = loads.index(min(loads))
        bins[owner].append(matrix)
        loads[owner] += PADDED[matrix]
    return bins, max(loads)


def placed(bins):
    where = {}
    for owner, group in enumerate(bins):
        offset = 0
        for matrix in group:
            where[matrix] = (owner, offset)
            offset += PADDED[matrix]
    return where


def turned(ref, scratch, total):
    value = ref[...].T
    if total > value.shape[1]:
        value = jnp.concatenate(
            [value, jnp.zeros((value.shape[0], total - value.shape[1]), value.dtype)], axis=1
        )
    scratch[...] = value


def part(matrix, wide, down_t, embed_t):
    if matrix == DOWN:
        return down_t[...]
    if matrix == EMBED:
        return embed_t[...]
    return wide[:, OFFSETS[matrix] : OFFSETS[matrix] + WIDTHS[matrix]]


def put_chunk(dst, group, wide, down_t, embed_t):
    offset = 0
    for matrix in group:
        dst[:, offset : offset + PADDED[matrix]] = part(matrix, wide, down_t, embed_t).astype(dst.dtype)
        offset += PADDED[matrix]
    if offset < dst.shape[1]:
        dst[:, offset:] = jnp.zeros((dst.shape[0], dst.shape[1] - offset), dst.dtype)


def split_kernel(bins, index, wide, down, embed, own, *rest):
    sends, (down_t, embed_t) = rest[:-2], rest[-2:]
    turned(down, down_t, PADDED[DOWN])
    turned(embed, embed_t, PADDED[EMBED])
    for k, dst in enumerate((own,) + sends):
        for target, group in enumerate(bins):

            @pl.when((index[0] ^ k) == target)
            def _():
                put_chunk(dst, group, wide, down_t, embed_t)


def sum_kernel(count, own, *rest):
    received, mom, g_out, y_out = rest[:count], rest[count], rest[count + 1], rest[count + 2]
    g = own[...]
    for piece in received:
        g = g + piece[...].astype(jnp.float32)
    g_out[...] = g.astype(jnp.bfloat16)
    y_out[...] = (g + MOMENTUM * (MOMENTUM * mom[...] + g)).astype(jnp.bfloat16)


def newton_kernel(bins, count, rows, index, *rest):
    pieces, out, x_ref = rest[:count], rest[count], rest[count + 1]
    piece_rows = pieces[0].shape[0]
    for number, piece in enumerate(pieces):
        x_ref[number * piece_rows : (number + 1) * piece_rows, :] = piece[...]

    def polynomial(x, scale):
        gram = lax.dot_general(x, x, (((1,), (1,)), ((), ())), preferred_element_type=jnp.float32)
        gram = (gram * scale * scale).astype(jnp.bfloat16)
        square = jnp.dot(gram, gram, preferred_element_type=jnp.float32)
        return (COEF_B * gram.astype(jnp.float32) + COEF_C * square).astype(jnp.bfloat16)

    def branch(group):
        spans = []
        offset = 0
        for matrix in group:
            spans.append((offset, PADDED[matrix], WIDTHS[matrix]))
            offset += PADDED[matrix]
        scales = []
        for offset, width, _ in spans:
            x = x_ref[:, offset : offset + width].astype(jnp.float32)
            scales.append(1.0 / (jnp.sqrt(jnp.sum(x * x)) + EPSILON))

        def step(number, scales):
            for (offset, width, _), scale in zip(spans, scales):
                x = x_ref[:, offset : offset + width]
                poly = polynomial(x, scale)
                x_ref[:, offset : offset + width] = (
                    scale
                    * (COEF_A * x.astype(jnp.float32) + jnp.dot(poly, x, preferred_element_type=jnp.float32))
                ).astype(jnp.bfloat16)
            return tuple(jnp.float32(1.0) for _ in scales)

        scales = lax.fori_loop(0, NS_ITERS - 1, step, tuple(scales))
        for (offset, width, true_width), scale in zip(spans, scales):
            x = x_ref[:, offset : offset + width]
            poly = polynomial(x, scale)
            factor = math.sqrt(max(D, true_width))
            out[:, offset : offset + width] = (
                (scale * factor)
                * (
                    COEF_A * x[:rows].astype(jnp.float32)
                    + jnp.dot(poly[:rows], x, preferred_element_type=jnp.float32)
                )
            ).astype(jnp.bfloat16)

    for target, group in enumerate(bins):
        if group:

            @pl.when(index[0] == target)
            def _():
                branch(group)


def per_index(bins, index, body):
    for mine in range(len(bins)):

        @pl.when(index[0] == mine)
        def _():
            body(mine)


def momentum_kernel(bins, index, wide, down, embed, *rest):
    n = len(bins)
    pieces, (new_wide, new_down, new_embed) = rest[:n], rest[n:]
    where = placed(bins)

    def body(mine):
        for matrix in range(6):
            owner, offset = where[matrix]
            g = pieces[mine ^ owner][:, offset : offset + PADDED[matrix]].astype(jnp.float32)
            if matrix == DOWN:
                new_down[...] = MOMENTUM * down[...] + g.T
            elif matrix == EMBED:
                new_embed[...] = MOMENTUM * embed[...] + g.T[:CLASSES]
            else:
                span = slice(OFFSETS[matrix], OFFSETS[matrix] + WIDTHS[matrix])
                new_wide[:, span] = MOMENTUM * wide[:, span] + g

    per_index(bins, index, body)


def update_kernel(bins, index, *rest):
    n = len(bins)
    pieces, (upd_wide, upd_down, upd_embed) = rest[:n], rest[n:]
    where = placed(bins)

    def body(mine):
        for matrix in range(6):
            owner, offset = where[matrix]
            value = pieces[mine ^ owner][:, offset : offset + PADDED[matrix]]
            if matrix == DOWN:
                upd_down[...] = value.astype(jnp.float32).T.astype(jnp.bfloat16)
            elif matrix == EMBED:
                upd_embed[...] = value.astype(jnp.float32).T[:CLASSES].astype(jnp.bfloat16)
            else:
                upd_wide[:, OFFSETS[matrix] : OFFSETS[matrix] + WIDTHS[matrix]] = value

    per_index(bins, index, body)


def call(kernel, outs, args, scratch=(), indexed=True, flops=0):
    vmem = pl.BlockSpec(memory_space=pltpu.VMEM)
    specs = [vmem] * len(args)
    if indexed:
        specs[0] = pl.BlockSpec(memory_space=pltpu.SMEM)
    size = sum(a.size * a.dtype.itemsize for a in args) + sum(
        math.prod(o.shape) * o.dtype.itemsize for o in outs
    )
    return pl.pallas_call(
        kernel,
        out_shape=tuple(outs),
        in_specs=specs,
        out_specs=tuple([vmem] * len(outs)),
        scratch_shapes=list(scratch),
        compiler_params=pltpu.CompilerParams(vmem_limit_bytes=VMEM_LIMIT),
        cost_estimate=pl.CostEstimate(flops=flops, bytes_accessed=size, transcendentals=0),
    )(*args)


def swap(value, axis, k, n):
    return lax.ppermute(value, axis, [(i, i ^ k) for i in range(n)])


def spread(value, axis, n):
    return [value] + [swap(value, axis, k, n) for k in range(1, n)]


def gather_rows(value, n):
    pieces = [value] + [swap(value, "shard", 2 * k, n) for k in range(1, n // 2)]
    return pieces + [swap(piece, "shard", 1, n) for piece in pieces]


def per_device(grad_wide, grad_down, grad_embed, mom_wide, mom_down, mom_embed):
    n_rep, n_shard = lax.axis_size("rep"), lax.axis_size("shard")
    bins, width = plan(n_rep)
    index = lax.axis_index("rep").astype(jnp.int32).reshape(1)
    grads = (grad_wide[0, 0], grad_down[0, 0], grad_embed[0])
    moms = (mom_wide[0], mom_down[0], mom_embed)
    rows = grads[0].shape[0]
    chunk32 = jax.ShapeDtypeStruct((rows, width), jnp.float32)
    chunk16 = jax.ShapeDtypeStruct((rows, width), jnp.bfloat16)
    turn = (pltpu.VMEM((rows, PADDED[DOWN]), jnp.float32), pltpu.VMEM((rows, PADDED[EMBED]), jnp.float32))

    own, *sends = call(
        functools.partial(split_kernel, bins), [chunk32] + [chunk16] * (n_rep - 1), (index,) + grads, turn
    )
    received = [swap(piece, "rep", k + 1, n_rep) for k, piece in enumerate(sends)]
    (mom_own,) = call(functools.partial(split_kernel, bins), [chunk32], (index,) + moms, turn)
    g, y = call(
        functools.partial(sum_kernel, n_rep - 1),
        [chunk16, chunk16],
        (own, *received, mom_own),
        indexed=False,
    )

    pieces = gather_rows(y, n_shard)
    g_all = spread(g, "rep", n_rep)
    news = call(
        functools.partial(momentum_kernel, bins),
        [jax.ShapeDtypeStruct(m.shape, jnp.float32) for m in moms],
        (index,) + moms + tuple(g_all),
    )
    if rows % 16:
        pieces = [jnp.concatenate(pieces, axis=0)]
    (upd,) = call(
        functools.partial(newton_kernel, bins, len(pieces), rows),
        [chunk16],
        (index,) + tuple(pieces),
        (pltpu.VMEM((D, width), jnp.bfloat16),),
        flops=NS_ITERS * (4 * D * D * width + 2 * D * D * D),
    )
    updates = call(
        functools.partial(update_kernel, bins),
        [jax.ShapeDtypeStruct(m.shape, jnp.bfloat16) for m in moms],
        (index,) + tuple(spread(upd, "rep", n_rep)),
    )
    return (news[0][None], news[1][None], news[2], updates[0][None], updates[1][None], updates[2])


def solution(mesh):
    placed_in = (
        P("rep", None, "shard", None),
        P("rep", None, None, "shard"),
        P("rep", None, "shard"),
        P(None, "shard", None),
        P(None, None, "shard"),
        P(None, "shard"),
    )
    return jax.shard_map(
        per_device,
        mesh=mesh,
        in_specs=placed_in,
        out_specs=placed_in[3:] + placed_in[3:],
        check_vma=False,
    )
```

```python
import functools
import math

import jax
import jax.numpy as jnp
from jax import lax
from jax.experimental import pallas as pl
from jax.experimental.pallas import tpu as pltpu
from jax.sharding import PartitionSpec as P

D = 384
MLP = 1536
ADA = 2304
CLASSES = 1001
NS_ITERS = 5
QKV = 1152

COEF_A = 3.4445
COEF_B = -4.775
COEF_C = 2.0315
MOMENTUM = 0.95
EPSILON = 1e-07

VMEM_LIMIT = 48 * 1024 * 1024

WIDTHS = [QKV, D, MLP, ADA, MLP, CLASSES]
OFFSETS = [0, QKV, QKV + D, QKV + D + MLP]
PADDED = [-(-width // 128) * 128 for width in WIDTHS]
DOWN, EMBED = 4, 5
TILE = 256


def plan(n_rep):
    bins = [[] for _ in range(n_rep)]
    loads = [0] * n_rep
    for matrix in sorted(range(6), key=lambda m: -PADDED[m]):
        owner = loads.index(min(loads))
        bins[owner].append(matrix)
        loads[owner] += PADDED[matrix]
    return bins, max(loads)


def placed(bins):
    where = {}
    for owner, group in enumerate(bins):
        offset = 0
        for matrix in group:
            where[matrix] = (owner, offset)
            offset += PADDED[matrix]
    return where


def part(matrix, wide, down, embed):
    if matrix == DOWN:
        return down[...]
    if matrix == EMBED:
        value = embed[...]
        tail = jnp.zeros((value.shape[0], PADDED[EMBED] - CLASSES), value.dtype)
        return jnp.concatenate([value, tail], axis=1)
    return wide[:, OFFSETS[matrix] : OFFSETS[matrix] + WIDTHS[matrix]]


def put_chunk(dst, group, wide, down, embed):
    offset = 0
    for matrix in group:
        dst[:, offset : offset + PADDED[matrix]] = part(matrix, wide, down, embed).astype(dst.dtype)
        offset += PADDED[matrix]
    if offset < dst.shape[1]:
        dst[:, offset:] = jnp.zeros((dst.shape[0], dst.shape[1] - offset), dst.dtype)


def split_kernel(bins, index, wide, down, embed, *outs):
    for k, dst in enumerate(outs):
        for target, group in enumerate(bins):

            @pl.when((index[0] ^ k) == target)
            def _():
                put_chunk(dst, group, wide, down, embed)


def sum_kernel(count, own, *rest):
    received, mom, g_out, y_out = rest[:count], rest[count], rest[count + 1], rest[count + 2]
    g = own[...]
    for piece in received:
        g = g + piece[...].astype(jnp.float32)
    g_out[...] = g.astype(jnp.bfloat16)
    y_out[...] = (g + MOMENTUM * (MOMENTUM * mom[...] + g)).astype(jnp.bfloat16)


def newton_kernel(bins, blocks, rows, index, *rest):
    count = sum(len(block) for block in blocks)
    pieces, out, x_ref, gram_ref = rest[:count], rest[-3], rest[-2], rest[-1]
    piece_rows = D // len(blocks)
    for number, block in enumerate(blocks):
        value = pieces[block[0]][...]
        for extra in block[1:]:
            value = value + pieces[extra][...]
        x_ref[number * piece_rows : (number + 1) * piece_rows, :] = value

    def outer(x):
        return lax.dot_general(x, x, (((1,), (1,)), ((), ())), preferred_element_type=jnp.float32)

    def branch(group):
        spans = []
        offset = 0
        for matrix in group:
            end = offset + PADDED[matrix]
            tiles = [slice(low, min(low + TILE, end)) for low in range(offset, end, TILE)]
            spans.append((tiles, math.sqrt(max(D, WIDTHS[matrix]))))
            offset = end

        diagonal = lax.broadcasted_iota(jnp.int32, (D, D), 0) == lax.broadcasted_iota(jnp.int32, (D, D), 1)
        scales = []
        for number, (tiles, _) in enumerate(spans):
            gram = jnp.zeros((D, D), jnp.float32)
            for tile in tiles:
                gram = gram + outer(x_ref[:, tile])
            gram_ref[number] = gram
            squares = jnp.sum(jnp.where(diagonal, gram, 0.0))
            scales.append(1.0 / (jnp.sqrt(squares) + EPSILON))

        def polynomial(number, scale):
            gram = (gram_ref[number] * scale * scale).astype(jnp.bfloat16)
            square = jnp.dot(gram, gram, preferred_element_type=jnp.float32)
            return COEF_B * gram.astype(jnp.float32) + COEF_C * square

        def step(_, scales):
            for number, ((tiles, _), scale) in enumerate(zip(spans, scales)):
                poly = (scale * polynomial(number, scale)).astype(jnp.bfloat16)
                gram = jnp.zeros((D, D), jnp.float32)
                for tile in tiles:
                    x = x_ref[:, tile]
                    x = (
                        (COEF_A * scale) * x.astype(jnp.float32)
                        + jnp.dot(poly, x, preferred_element_type=jnp.float32)
                    ).astype(jnp.bfloat16)
                    x_ref[:, tile] = x
                    gram = gram + outer(x)
                gram_ref[number] = gram
            return tuple(jnp.float32(1.0) for _ in scales)

        scales = lax.fori_loop(0, NS_ITERS - 1, step, tuple(scales))
        for number, ((tiles, factor), scale) in enumerate(zip(spans, scales)):
            factor = factor * scale
            poly = polynomial(number, scale)[:rows].astype(jnp.bfloat16)
            for tile in tiles:
                x = x_ref[:, tile]
                out[:, tile] = (
                    factor
                    * (COEF_A * x[:rows].astype(jnp.float32) + jnp.dot(poly, x, preferred_element_type=jnp.float32))
                ).astype(jnp.bfloat16)

    for target, group in enumerate(bins):
        if group:

            @pl.when(index[0] == target)
            def _():
                branch(group)


def per_index(bins, index, body):
    for mine in range(len(bins)):

        @pl.when(index[0] == mine)
        def _():
            body(mine)


def momentum_kernel(bins, index, wide, down, embed, *rest):
    n = len(bins)
    pieces, (new_wide, new_down, new_embed) = rest[:n], rest[n:]
    where = placed(bins)

    def body(mine):
        for matrix in range(6):
            owner, offset = where[matrix]
            g = pieces[mine ^ owner][:, offset : offset + PADDED[matrix]].astype(jnp.float32)
            if matrix == DOWN:
                new_down[...] = MOMENTUM * down[...] + g
            elif matrix == EMBED:
                new_embed[...] = MOMENTUM * embed[...] + g[:, :CLASSES]
            else:
                span = slice(OFFSETS[matrix], OFFSETS[matrix] + WIDTHS[matrix])
                new_wide[:, span] = MOMENTUM * wide[:, span] + g

    per_index(bins, index, body)


def update_kernel(bins, index, *rest):
    n = len(bins)
    pieces, (upd_wide, upd_down, upd_embed) = rest[:n], rest[n:]
    where = placed(bins)

    def body(mine):
        for matrix in range(6):
            owner, offset = where[matrix]
            value = pieces[mine ^ owner][:, offset : offset + PADDED[matrix]]
            if matrix == DOWN:
                upd_down[...] = value
            elif matrix == EMBED:
                upd_embed[...] = value[:, :CLASSES]
            else:
                upd_wide[:, OFFSETS[matrix] : OFFSETS[matrix] + WIDTHS[matrix]] = value

    per_index(bins, index, body)


def call(kernel, outs, args, scratch=(), indexed=True, flops=0, tied=0):
    vmem = pl.BlockSpec(memory_space=pltpu.VMEM)
    specs = [vmem] * (len(args) - tied) + [pl.BlockSpec(memory_space=pl.ANY)] * tied
    if indexed:
        specs[0] = pl.BlockSpec(memory_space=pltpu.SMEM)
    size = sum(a.size * a.dtype.itemsize for a in args) + sum(
        math.prod(o.shape) * o.dtype.itemsize for o in outs
    )
    return pl.pallas_call(
        kernel,
        out_shape=tuple(outs),
        in_specs=specs,
        out_specs=tuple([vmem] * len(outs)),
        scratch_shapes=list(scratch),
        compiler_params=pltpu.CompilerParams(vmem_limit_bytes=VMEM_LIMIT),
        cost_estimate=pl.CostEstimate(flops=flops, bytes_accessed=size, transcendentals=0),
    )(*args)


def swap(value, axis, k, n):
    return lax.ppermute(value, axis, [(i, i ^ k) for i in range(n)])


def spread(value, axis, n):
    return [swap(value, axis, k, n) for k in range(1, n)]


def along(value, hops):
    return lax.ppermute(value, "shard", [(2 * a + c, 2 * b + c) for a, b in hops for c in range(2)])


def gather_rows(value, n):
    if n == 8:
        far = along(value, [(0, 2), (2, 0), (1, 3), (3, 1)])
        near = along(value, [(0, 1), (1, 0), (2, 3), (3, 2)])
        middle = along(value, [(1, 2), (2, 1)])
        ends = along(far, [(2, 3), (1, 0)])
        pieces = [value, near, far, middle, ends]
        blocks = [[0], [1], [2], [3, 4]]
    else:
        pieces = [value] + [swap(value, "shard", 2 * k, n) for k in range(1, n // 2)]
        blocks = [[number] for number in range(n // 2)]
    count = len(pieces)
    pieces = pieces + [swap(piece, "shard", 1, n) for piece in pieces]
    return pieces, blocks + [[number + count for number in block] for block in blocks]


def per_device(grad_wide, grad_down, grad_embed, mom_wide, mom_down, mom_embed):
    n_rep, n_shard = lax.axis_size("rep"), lax.axis_size("shard")
    bins, width = plan(n_rep)
    index = lax.axis_index("rep").astype(jnp.int32).reshape(1)
    grads = (grad_wide[0, 0], grad_down[0, 0].T, grad_embed[0].T)
    moms = (mom_wide[0], mom_down[0].T, mom_embed.T)
    rows = grads[0].shape[0]
    chunk32 = jax.ShapeDtypeStruct((rows, width), jnp.float32)
    chunk16 = jax.ShapeDtypeStruct((rows, width), jnp.bfloat16)
    split = functools.partial(split_kernel, bins)

    own, *sends = call(split, [chunk32] + [chunk16] * (n_rep - 1), (index,) + grads)
    received = [swap(piece, "rep", k + 1, n_rep) for k, piece in enumerate(sends)]
    (mom_own,) = call(split, [chunk32], (index,) + moms)
    g, y = call(
        functools.partial(sum_kernel, n_rep - 1),
        [chunk16, chunk16],
        (own, *received, mom_own),
        indexed=False,
    )

    pieces, blocks = gather_rows(y, n_shard)
    g_others = spread(g, "rep", n_rep)
    if rows % 16:
        pieces = [jnp.concatenate(pieces, axis=0)]
        blocks = [[0]]
    (upd,) = call(
        functools.partial(newton_kernel, bins, blocks, rows),
        [chunk16],
        (index, *pieces, *g_others),
        (pltpu.VMEM((D, width), jnp.bfloat16), pltpu.VMEM((2, D, D), jnp.float32)),
        flops=NS_ITERS * (4 * D * D * width + 2 * D * D * D),
        tied=len(g_others),
    )
    upd_others = spread(upd, "rep", n_rep)
    news = call(
        functools.partial(momentum_kernel, bins),
        [jax.ShapeDtypeStruct(m.shape, jnp.float32) for m in moms],
        (index, *moms, g, *g_others),
    )
    updates = call(
        functools.partial(update_kernel, bins),
        [jax.ShapeDtypeStruct(m.shape, jnp.bfloat16) for m in moms],
        (index, upd, *upd_others),
    )
    return (
        news[0][None],
        news[1].T[None],
        news[2].T,
        updates[0][None],
        updates[1].T[None],
        updates[2].T,
    )


def solution(mesh):
    placed_in = (
        P("rep", None, "shard", None),
        P("rep", None, None, "shard"),
        P("rep", None, "shard"),
        P(None, "shard", None),
        P(None, None, "shard"),
        P(None, "shard"),
    )
    return jax.shard_map(
        per_device,
        mesh=mesh,
        in_specs=placed_in,
        out_specs=placed_in[3:] + placed_in[3:],
        check_vma=False,
    )
```

```python
import functools
import math

import jax
import jax.numpy as jnp
from jax import lax
from jax.experimental import pallas as pl
from jax.experimental.pallas import tpu as pltpu
from jax.sharding import PartitionSpec as P

D = 384
MLP = 1536
ADA = 2304
CLASSES = 1001
NS_ITERS = 5
QKV = 1152

COEF_A = 3.4445
COEF_B = -4.775
COEF_C = 2.0315
MOMENTUM = 0.95
EPSILON = 1e-07

VMEM_LIMIT = 48 * 1024 * 1024
VMEM_ALL = 63 * 1024 * 1024

WIDTHS = [QKV, D, MLP, ADA, MLP, CLASSES]
OFFSETS = [0, QKV, QKV + D, QKV + D + MLP]
PADDED = [-(-width // 128) * 128 for width in WIDTHS]
DOWN, EMBED = 4, 5
TILE = 256


def plan(n_rep):
    bins = [[] for _ in range(n_rep)]
    loads = [0] * n_rep
    for matrix in sorted(range(6), key=lambda m: -PADDED[m]):
        owner = loads.index(min(loads))
        bins[owner].append(matrix)
        loads[owner] += PADDED[matrix]
    return bins, max(loads)


def placed(bins):
    where = {}
    for owner, group in enumerate(bins):
        offset = 0
        for matrix in group:
            where[matrix] = (owner, offset)
            offset += PADDED[matrix]
    return where


def window(group, low, high):
    found = []
    offset = 0
    for matrix in group:
        first, last = max(low - offset, 0), min(high - offset, WIDTHS[matrix])
        if first < last:
            found.append((matrix, first, last, offset + first - low))
        offset += PADDED[matrix]
    return found


def source(matrix, first, last, wide, down, embed):
    if matrix == DOWN:
        return down.at[:, first:last]
    if matrix == EMBED:
        return embed.at[:, first:last]
    return wide.at[:, OFFSETS[matrix] + first : OFFSETS[matrix] + last]


def split_kernel(bins, low, high, index, wide, down, embed, *rest):
    outs, sems = rest[:-3], rest[-1]
    held, held_embed = rest[-3], rest[-2]
    copies = []
    for target, group in enumerate(bins):
        for matrix, first, last, place in window(group, low, high):
            if matrix == EMBED:
                dst = held_embed.at[:, first:last] if last < CLASSES or first > 0 else held_embed
                src = embed if dst is held_embed else source(matrix, first, last, wide, down, embed)
            else:
                dst = held.at[target, :, place : place + last - first]
                src = source(matrix, first, last, wide, down, embed)
            copy = pltpu.make_async_copy(src, dst, sems.at[len(copies)])
            copy.start()
            copies.append(copy)
    for copy in copies:
        copy.wait()
    for target, group in enumerate(bins):
        for matrix, first, last, place in window(group, low, high):
            if matrix == EMBED:
                held[target, :, place : place + last - first] = held_embed[:, first:last]
    for k, dst in enumerate(outs):
        for target, group in enumerate(bins):

            @pl.when((index[0] ^ k) == target)
            def _():
                end = 0
                for _, first, last, place in window(group, low, high):
                    dst[:, place : place + last - first] = held[target, :, place : place + last - first].astype(
                        dst.dtype
                    )
                    end = place + last - first
                if end < high - low:
                    dst[:, end:] = jnp.zeros((dst.shape[0], high - low - end), dst.dtype)


def sum_kernel(count, own, *rest):
    received, mom, g_out, y_out = rest[:count], rest[count], rest[count + 1], rest[count + 2]
    g = own[...]
    for piece in received:
        g = g + piece[...].astype(jnp.float32)
    g_out[...] = g.astype(jnp.bfloat16)
    y_out[...] = (g + MOMENTUM * (MOMENTUM * mom[...] + g)).astype(jnp.bfloat16)


def join_kernel(left, right, *rest):
    out, half = rest[-1], left.shape[1]
    out[:, :half] = left[...]
    out[:, half:] = right[...]


def newton_kernel(bins, count, halves, rows, index, *rest):
    pieces, out, x_ref = rest[: count * halves], rest[-2], rest[-1]
    piece_rows, piece_width = pieces[0].shape
    for half in range(halves):
        for number in range(count):
            x_ref[
                number * piece_rows : (number + 1) * piece_rows,
                half * piece_width : (half + 1) * piece_width,
            ] = pieces[half * count + number][...]

    def branch(group):
        spans = []
        offset = 0
        for matrix in group:
            end = offset + PADDED[matrix]
            tiles = [slice(low, min(low + TILE, end)) for low in range(offset, end, TILE)]
            spans.append((slice(offset, end), tiles, math.sqrt(max(D, WIDTHS[matrix]))))
            offset = end

        def outer(span):
            x = x_ref[:, span]
            return lax.dot_general(x, x, (((1,), (1,)), ((), ())), preferred_element_type=jnp.float32)

        def polynomial(gram):
            gram = gram.astype(jnp.bfloat16)
            square = jnp.dot(gram, gram, preferred_element_type=jnp.float32)
            return COEF_B * gram.astype(jnp.float32) + COEF_C * square

        def advance(tiles, poly, factor):
            for tile in tiles:
                x = x_ref[:, tile]
                x_ref[:, tile] = (
                    factor * x.astype(jnp.float32) + jnp.dot(poly, x, preferred_element_type=jnp.float32)
                ).astype(jnp.bfloat16)

        diagonal = lax.broadcasted_iota(jnp.int32, (D, D), 0) == lax.broadcasted_iota(jnp.int32, (D, D), 1)
        for span, tiles, _ in spans:
            gram = outer(span)
            scale = 1.0 / (jnp.sqrt(jnp.sum(jnp.where(diagonal, gram, 0.0))) + EPSILON)
            poly = (scale * polynomial(gram * scale * scale)).astype(jnp.bfloat16)
            advance(tiles, poly, COEF_A * scale)

        def step(_, carry):
            polys = [polynomial(outer(span)).astype(jnp.bfloat16) for span, _, _ in spans]
            for poly, (_, tiles, _) in zip(polys, spans):
                advance(tiles, poly, COEF_A)
            return carry

        lax.fori_loop(0, NS_ITERS - 2, step, 0)
        for span, tiles, factor in spans:
            poly = polynomial(outer(span))[:rows].astype(jnp.bfloat16)
            for tile in tiles:
                x = x_ref[:, tile]
                out[:, tile] = (
                    factor
                    * (COEF_A * x[:rows].astype(jnp.float32) + jnp.dot(poly, x, preferred_element_type=jnp.float32))
                ).astype(jnp.bfloat16)

    for target, group in enumerate(bins):
        if group:

            @pl.when(index[0] == target)
            def _():
                branch(group)


def per_index(bins, index, body):
    for mine in range(len(bins)):

        @pl.when(index[0] == mine)
        def _():
            body(mine)


def momentum_kernel(bins, index, wide, down, embed, *rest):
    n = len(bins)
    pieces, (new_wide, new_down, new_embed) = rest[:n], rest[n:]
    where = placed(bins)

    def body(mine):
        for matrix in range(6):
            owner, offset = where[matrix]
            g = pieces[mine ^ owner][:, offset : offset + PADDED[matrix]].astype(jnp.float32)
            if matrix == DOWN:
                new_down[...] = MOMENTUM * down[...] + g
            elif matrix == EMBED:
                new_embed[...] = MOMENTUM * embed[...] + g[:, :CLASSES]
            else:
                span = slice(OFFSETS[matrix], OFFSETS[matrix] + WIDTHS[matrix])
                new_wide[:, span] = MOMENTUM * wide[:, span] + g

    per_index(bins, index, body)


def update_kernel(bins, index, *rest):
    n = len(bins)
    pieces, (upd_wide, upd_down, upd_embed) = rest[:n], rest[n:]
    where = placed(bins)

    def body(mine):
        for matrix in range(6):
            owner, offset = where[matrix]
            value = pieces[mine ^ owner][:, offset : offset + PADDED[matrix]]
            if matrix == DOWN:
                upd_down[...] = value
            elif matrix == EMBED:
                upd_embed[...] = value[:, :CLASSES]
            else:
                upd_wide[:, OFFSETS[matrix] : OFFSETS[matrix] + WIDTHS[matrix]] = value

    per_index(bins, index, body)


def call(kernel, outs, args, scratch=(), indexed=True, flops=0, tied=0, held=0):
    specs = [pl.BlockSpec(memory_space=pltpu.SMEM)] if indexed else []
    specs += [pl.BlockSpec(memory_space=pltpu.MemorySpace.HBM)] * held
    specs += [pl.BlockSpec(memory_space=pltpu.VMEM)] * (len(args) - tied - len(specs))
    specs += [pl.BlockSpec(memory_space=pl.ANY)] * tied
    size = sum(a.size * a.dtype.itemsize for a in args) + sum(
        math.prod(o.shape) * o.dtype.itemsize for o in outs
    )
    return pl.pallas_call(
        kernel,
        out_shape=tuple(outs),
        in_specs=specs,
        out_specs=tuple([pl.BlockSpec(memory_space=pltpu.VMEM)] * len(outs)),
        scratch_shapes=list(scratch),
        compiler_params=pltpu.CompilerParams(vmem_limit_bytes=VMEM_ALL if held else VMEM_LIMIT),
        cost_estimate=pl.CostEstimate(flops=flops, bytes_accessed=size, transcendentals=0),
    )(*args)


def split(bins, low, high, index, arrays, dtypes):
    rows = arrays[0].shape[0]
    scratch = (
        pltpu.VMEM((len(bins), rows, high - low), jnp.float32),
        pltpu.VMEM((rows, CLASSES), jnp.float32),
        pltpu.SemaphoreType.DMA((8 + len(bins),)),
    )
    outs = [jax.ShapeDtypeStruct((rows, high - low), dtype) for dtype in dtypes]
    return call(functools.partial(split_kernel, bins, low, high), outs, (index, *arrays), scratch, held=3)


def swap(value, axis, k, n):
    return lax.ppermute(value, axis, [(i, i ^ k) for i in range(n)])


def spread(value, axis, n):
    return [swap(value, axis, k, n) for k in range(1, n)]


def gather_rows(value, n):
    pieces = [value] + [swap(value, "shard", k, n) for k in range(2, n, 2)]
    return pieces + [swap(piece, "shard", 1, n) for piece in pieces]


def per_device(grad_wide, grad_down, grad_embed, mom_wide, mom_down, mom_embed):
    n_rep, n_shard = lax.axis_size("rep"), lax.axis_size("shard")
    bins, width = plan(n_rep)
    index = lax.axis_index("rep").astype(jnp.int32).reshape(1)
    grads = (grad_wide[0, 0], grad_down[0, 0].T, grad_embed[0].T)
    moms = (mom_wide[0], mom_down[0].T, mom_embed.T)
    rows = grads[0].shape[0]
    whole = jax.ShapeDtypeStruct((rows, width), jnp.bfloat16)
    windows = [(0, width // 2), (width // 2, width)]

    split_grads = [
        split(bins, low, high, index, grads, [jnp.float32] + [jnp.bfloat16] * (n_rep - 1)) for low, high in windows
    ]
    received = [[swap(piece, "rep", k + 1, n_rep) for k, piece in enumerate(own[1:])] for own in split_grads]
    gs, pieces = [], []
    for half, (low, high) in enumerate(windows):
        (mom_own,) = split(bins, low, high, index, moms, [jnp.float32])
        g, y = call(
            functools.partial(sum_kernel, n_rep - 1),
            [jax.ShapeDtypeStruct((rows, high - low), jnp.bfloat16)] * 2,
            (split_grads[half][0], *received[half], mom_own),
            indexed=False,
        )
        gs.append(g)
        pieces.append(gather_rows(y, n_shard))
    (g,) = call(join_kernel, [whole], (*gs, pieces[0][1]), indexed=False, tied=1)
    g_others = spread(g, "rep", n_rep)
    if rows % 16:
        pieces = [[jnp.concatenate(half, axis=0)] for half in pieces]
    (upd,) = call(
        functools.partial(newton_kernel, bins, len(pieces[0]), len(pieces), rows),
        [whole],
        (index, *pieces[0], *pieces[1], *g_others),
        (pltpu.VMEM((D, width), jnp.bfloat16),),
        flops=NS_ITERS * (4 * D * D * width + 2 * D * D * D),
        tied=len(g_others),
    )
    upd_others = spread(upd, "rep", n_rep)
    news = call(
        functools.partial(momentum_kernel, bins),
        [jax.ShapeDtypeStruct(m.shape, jnp.float32) for m in moms],
        (index, *moms, g, *g_others),
    )
    updates = call(
        functools.partial(update_kernel, bins),
        [jax.ShapeDtypeStruct(m.shape, jnp.bfloat16) for m in moms],
        (index, upd, *upd_others),
    )
    return (
        news[0][None],
        news[1].T[None],
        news[2].T,
        updates[0][None],
        updates[1].T[None],
        updates[2].T,
    )


def solution(mesh):
    placed_in = (
        P("rep", None, "shard", None),
        P("rep", None, None, "shard"),
        P("rep", None, "shard"),
        P(None, "shard", None),
        P(None, None, "shard"),
        P(None, "shard"),
    )
    return jax.shard_map(
        per_device,
        mesh=mesh,
        in_specs=placed_in,
        out_specs=placed_in[3:] + placed_in[3:],
        check_vma=False,
    )
```

```python
import functools
import math

import jax
import jax.numpy as jnp
from jax import lax
from jax.experimental import pallas as pl
from jax.experimental.pallas import tpu as pltpu
from jax.sharding import PartitionSpec as P

D = 384
MLP = 1536
ADA = 2304
CLASSES = 1001
NS_ITERS = 5
QKV = 1152

COEF_A = 3.4445
COEF_B = -4.775
COEF_C = 2.0315
MOMENTUM = 0.95
EPSILON = 1e-07

VMEM_LIMIT = 48 * 1024 * 1024
VMEM_ALL = 63 * 1024 * 1024

WIDTHS = [QKV, D, MLP, ADA, MLP, CLASSES]
OFFSETS = [0, QKV, QKV + D, QKV + D + MLP]
PADDED = [-(-width // 128) * 128 for width in WIDTHS]
DOWN, EMBED = 4, 5
TILE = 256


def plan(n_rep):
    bins = [[] for _ in range(n_rep)]
    loads = [0] * n_rep
    for matrix in sorted(range(6), key=lambda m: -PADDED[m]):
        owner = loads.index(min(loads))
        bins[owner].append(matrix)
        loads[owner] += PADDED[matrix]
    return bins, max(loads)


def layout(bins):
    found = []
    for owner, group in enumerate(bins):
        offset = 0
        for matrix in group:
            found.append((matrix, owner, offset))
            offset += PADDED[matrix]
    return found


def source(matrix, wide, down, embed):
    if matrix == DOWN:
        return down
    if matrix == EMBED:
        return embed
    return wide.at[:, OFFSETS[matrix] : OFFSETS[matrix] + WIDTHS[matrix]]


def split_kernel(bins, wide, down, embed, out, held, held_embed, sems):
    parts = sorted(layout(bins), key=lambda p: -WIDTHS[p[0]])
    copies = []
    for number, (matrix, owner, offset) in enumerate(parts):
        span = slice(offset, offset + WIDTHS[matrix])
        dst = held_embed if matrix == EMBED else held.at[owner, :, span]
        copies.append(pltpu.make_async_copy(source(matrix, wide, down, embed), dst, sems.at[number]))
        copies[-1].start()
    for copy, (matrix, owner, offset) in zip(copies, parts):
        copy.wait()
        span = slice(offset, offset + WIDTHS[matrix])
        if matrix == EMBED:
            value = held_embed[...]
            out[owner, :, offset : offset + PADDED[matrix]] = jnp.concatenate(
                [value, jnp.zeros((value.shape[0], PADDED[EMBED] - CLASSES), value.dtype)], axis=1
            ).astype(out.dtype)
        else:
            out[owner, :, span] = held[owner, :, span].astype(out.dtype)
    for owner, group in enumerate(bins):
        end = sum(PADDED[matrix] for matrix in group)
        if end < out.shape[2]:
            out[owner, :, end:] = jnp.zeros((out.shape[1], out.shape[2] - end), out.dtype)


def sum_kernel(bins, copies_z, index, received, wide, down, embed, g_out, y_out):
    n = received.shape[0]

    def body(group):
        offset = 0
        for matrix in group:
            span = slice(offset, offset + PADDED[matrix])
            if matrix == DOWN:
                mom = down[...]
            elif matrix == EMBED:
                mom = embed[...]
                mom = jnp.concatenate(
                    [mom, jnp.zeros((mom.shape[0], PADDED[EMBED] - CLASSES), mom.dtype)], axis=1
                )
            else:
                mom = wide[:, OFFSETS[matrix] : OFFSETS[matrix] + WIDTHS[matrix]]
            g = received[0, :, span].astype(jnp.float32)
            for number in range(1, n):
                g = g + received[number, :, span].astype(jnp.float32)
            y = (g + MOMENTUM * (MOMENTUM * mom + g)).astype(jnp.bfloat16)
            g = g.astype(jnp.bfloat16)
            for number in range(n):
                g_out[number, :, span] = g
            for number in range(copies_z):
                y_out[number, :, span] = y
            offset += PADDED[matrix]
        if offset < g_out.shape[2]:
            zeros = jnp.zeros((g_out.shape[1], g_out.shape[2] - offset), jnp.bfloat16)
            for number in range(n):
                g_out[number, :, offset:] = zeros
            for number in range(copies_z):
                y_out[number, :, offset:] = zeros

    for target, group in enumerate(bins):

        @pl.when(index[0] == target)
        def _():
            body(group)


def newton_kernel(bins, copies, index, same, other, *rest):
    out, x_ref, poly_ref = rest[-3:]
    half, rows = D // 2, out.shape[1]
    x_ref[:half, :] = same[...]
    x_ref[half:, :] = other[...]
    mine = pl.ds(0, D) if rows == D else pl.ds(pl.multiple_of(index[1] * rows, rows), rows)

    def branch(group):
        spans = []
        offset = 0
        for matrix in group:
            end = offset + PADDED[matrix]
            tiles = [slice(low, min(low + TILE, end)) for low in range(offset, end, TILE)]
            spans.append((slice(offset, end), tiles, math.sqrt(max(D, WIDTHS[matrix]))))
            offset = end

        def outer(span):
            x = x_ref[:, span]
            return lax.dot_general(x, x, (((1,), (1,)), ((), ())), preferred_element_type=jnp.float32)

        def polynomial(gram):
            gram = gram.astype(jnp.bfloat16)
            square = jnp.dot(gram, gram, preferred_element_type=jnp.float32)
            return COEF_B * gram.astype(jnp.float32) + COEF_C * square

        def advance(tiles, poly, factor):
            for tile in tiles:
                x = x_ref[:, tile]
                x_ref[:, tile] = (
                    factor * x.astype(jnp.float32) + jnp.dot(poly, x, preferred_element_type=jnp.float32)
                ).astype(jnp.bfloat16)

        diagonal = lax.broadcasted_iota(jnp.int32, (D, D), 0) == lax.broadcasted_iota(jnp.int32, (D, D), 1)
        for span, tiles, _ in spans:
            gram = outer(span)
            scale = 1.0 / (jnp.sqrt(jnp.sum(jnp.where(diagonal, gram, 0.0))) + EPSILON)
            poly = (scale * polynomial(gram * scale * scale)).astype(jnp.bfloat16)
            advance(tiles, poly, COEF_A * scale)

        def step(_, carry):
            polys = [polynomial(outer(span)).astype(jnp.bfloat16) for span, _, _ in spans]
            for poly, (_, tiles, _) in zip(polys, spans):
                advance(tiles, poly, COEF_A)
            return carry

        lax.fori_loop(0, NS_ITERS - 2, step, 0)
        for span, tiles, factor in spans:
            poly_ref[...] = polynomial(outer(span)).astype(jnp.bfloat16)
            poly = poly_ref[mine, :]
            for tile in tiles:
                value = (
                    factor
                    * (
                        COEF_A * x_ref[mine, tile].astype(jnp.float32)
                        + jnp.dot(poly, x_ref[:, tile], preferred_element_type=jnp.float32)
                    )
                ).astype(jnp.bfloat16)
                for number in range(copies):
                    out[number, :, tile] = value

    for target, group in enumerate(bins):
        if group:

            @pl.when(index[0] == target)
            def _():
                branch(group)


def momentum_kernel(bins, gathered, wide, down, embed, new_wide, new_down, new_embed):
    for matrix, owner, offset in layout(bins):
        g = gathered[owner, :, offset : offset + PADDED[matrix]].astype(jnp.float32)
        if matrix == DOWN:
            new_down[...] = MOMENTUM * down[...] + g
        elif matrix == EMBED:
            new_embed[...] = MOMENTUM * embed[...] + g[:, :CLASSES]
        else:
            span = slice(OFFSETS[matrix], OFFSETS[matrix] + WIDTHS[matrix])
            new_wide[:, span] = MOMENTUM * wide[:, span] + g


def update_kernel(bins, gathered, upd_wide, upd_down, upd_embed):
    for matrix, owner, offset in layout(bins):
        value = gathered[owner, :, offset : offset + PADDED[matrix]]
        if matrix == DOWN:
            upd_down[...] = value
        elif matrix == EMBED:
            upd_embed[...] = value[:, :CLASSES]
        else:
            upd_wide[:, OFFSETS[matrix] : OFFSETS[matrix] + WIDTHS[matrix]] = value


VMEM = pl.BlockSpec(memory_space=pltpu.VMEM)
SMEM = pl.BlockSpec(memory_space=pltpu.SMEM)
ANY = pl.BlockSpec(memory_space=pl.ANY)


def call(kernel, outs, args, specs, scratch=(), flops=0, limit=VMEM_LIMIT):
    size = sum(a.size * a.dtype.itemsize for a in args) + sum(
        math.prod(o.shape) * o.dtype.itemsize for o in outs
    )
    return pl.pallas_call(
        kernel,
        out_shape=tuple(outs),
        in_specs=specs,
        out_specs=tuple([VMEM] * len(outs)),
        scratch_shapes=list(scratch),
        compiler_params=pltpu.CompilerParams(vmem_limit_bytes=limit),
        cost_estimate=pl.CostEstimate(flops=flops, bytes_accessed=size, transcendentals=0),
    )(*args)


def exchange(value, axis, groups=None):
    return lax.all_to_all(value, axis, 0, 0, axis_index_groups=groups)


def per_device(grad_wide, grad_down, grad_embed, mom_wide, mom_down, mom_embed):
    n_rep, n_shard = lax.axis_size("rep"), lax.axis_size("shard")
    chips = n_shard // 2
    bins, width = plan(n_rep)
    index = jnp.stack([lax.axis_index("rep"), lax.axis_index("shard") // 2]).astype(jnp.int32)
    grads = (grad_wide[0, 0], grad_down[0, 0].T, grad_embed[0].T)
    moms = (mom_wide[0], mom_down[0].T, mom_embed.T)
    rows = grads[0].shape[0]

    def stacked(count):
        return jax.ShapeDtypeStruct((count, rows, width), jnp.bfloat16)

    (sends,) = call(
        functools.partial(split_kernel, bins),
        [stacked(n_rep)],
        grads,
        [ANY] * 3,
        (
            pltpu.VMEM((n_rep, rows, width), jnp.float32),
            pltpu.VMEM((rows, CLASSES), jnp.float32),
            pltpu.SemaphoreType.DMA((6,)),
        ),
        limit=VMEM_ALL,
    )
    g, y = call(
        functools.partial(sum_kernel, bins, chips),
        [stacked(n_rep), stacked(chips)],
        (index, exchange(sends, "rep"), *moms),
        [SMEM] + [VMEM] * 4,
    )
    groups = [[2 * chip + core for chip in range(chips)] for core in range(2)]
    same = exchange(y, "shard", groups).reshape(chips * rows, width)
    other = lax.ppermute(same, "shard", [(i, i ^ 1) for i in range(n_shard)])
    g_all = exchange(g, "rep")
    aligned = rows % 16 == 0
    (upd,) = call(
        functools.partial(newton_kernel, bins, n_rep if aligned else 1),
        [stacked(n_rep) if aligned else jax.ShapeDtypeStruct((1, D, width), jnp.bfloat16)],
        (index, same, other, g_all),
        [SMEM, VMEM, VMEM, ANY],
        (pltpu.VMEM((D, width), jnp.bfloat16), pltpu.VMEM((D, D), jnp.bfloat16)),
        flops=NS_ITERS * (4 * D * D * width + 2 * D * D * D),
    )
    if not aligned:
        upd = lax.dynamic_slice_in_dim(upd, index[1] * rows, rows, 1)
        upd = jnp.broadcast_to(upd, (n_rep, rows, width))
    upd_all = exchange(upd, "rep")
    news = call(
        functools.partial(momentum_kernel, bins),
        [jax.ShapeDtypeStruct(m.shape, jnp.float32) for m in moms],
        (g_all, *moms),
        [VMEM] * 4,
    )
    updates = call(
        functools.partial(update_kernel, bins),
        [jax.ShapeDtypeStruct(m.shape, jnp.bfloat16) for m in moms],
        (upd_all,),
        [VMEM],
    )
    return (
        news[0][None],
        news[1].T[None],
        news[2].T,
        updates[0][None],
        updates[1].T[None],
        updates[2].T,
    )


def solution(mesh):
    placed_in = (
        P("rep", None, "shard", None),
        P("rep", None, None, "shard"),
        P("rep", None, "shard"),
        P(None, "shard", None),
        P(None, None, "shard"),
        P(None, "shard"),
    )
    return jax.shard_map(
        per_device,
        mesh=mesh,
        in_specs=placed_in,
        out_specs=placed_in[3:] + placed_in[3:],
        check_vma=False,
    )
```

```python
import functools
import math

import jax
import jax.numpy as jnp
from jax import lax
from jax.experimental import pallas as pl
from jax.experimental.pallas import tpu as pltpu
from jax.sharding import PartitionSpec as P

D = 384
MLP = 1536
ADA = 2304
CLASSES = 1001
NS_ITERS = 5
QKV = 1152

COEF_A = 3.4445
COEF_B = -4.775
COEF_C = 2.0315
MOMENTUM = 0.95
EPSILON = 1e-07

VMEM_LIMIT = 48 * 1024 * 1024
VMEM_ALL = 63 * 1024 * 1024

WIDTHS = [QKV, D, MLP, ADA, MLP, CLASSES]
OFFSETS = [0, QKV, QKV + D, QKV + D + MLP]
PADDED = [-(-width // 128) * 128 for width in WIDTHS]
DOWN, EMBED = 4, 5
TILE = 256


def plan(n_rep):
    bins = [[] for _ in range(n_rep)]
    loads = [0] * n_rep
    for matrix in sorted(range(6), key=lambda m: -PADDED[m]):
        owner = loads.index(min(loads))
        bins[owner].append(matrix)
        loads[owner] += PADDED[matrix]
    return bins, max(loads)


def window(group, low, high):
    found = []
    offset = 0
    for matrix in group:
        first, last = max(low - offset, 0), min(high - offset, PADDED[matrix])
        if first < last:
            found.append((matrix, first, offset + first - low, last - first))
        offset += PADDED[matrix]
    return found


def columns(matrix, first, width, wide, down, embed):
    if matrix == DOWN:
        return down[:, first : first + width]
    if matrix == EMBED:
        last = min(first + width, CLASSES)
        value = embed[:, first:last]
        if last < first + width:
            tail = jnp.zeros((value.shape[0], first + width - last), value.dtype)
            value = jnp.concatenate([value, tail], axis=1)
        return value
    return wide[:, OFFSETS[matrix] + first : OFFSETS[matrix] + first + width]


def split_kernel(bins, windows, index, wide, down, embed, *rest):
    n = len(bins)
    outs, held, sems = rest[: len(windows) * n], rest[-4:-1], rest[-1]
    copies = [pltpu.make_async_copy(src, dst, sems.at[i]) for i, (src, dst) in enumerate(zip((wide, down, embed), held))]
    for copy in copies:
        copy.start()
    for copy in copies:
        copy.wait()
    for half, (low, high) in enumerate(windows):
        for k in range(n):
            dst = outs[half * n + k]
            for target, group in enumerate(bins):

                @pl.when((index[0] ^ k) == target)
                def _():
                    end = 0
                    for matrix, first, place, width in window(group, low, high):
                        dst[:, place : place + width] = columns(matrix, first, width, *held).astype(dst.dtype)
                        end = place + width
                    if end < high - low:
                        dst[:, end:] = jnp.zeros((dst.shape[0], high - low - end), dst.dtype)


def own_kernel(bins, index, wide, down, embed, out):
    for target, group in enumerate(bins):

        @pl.when(index[0] == target)
        def _():
            end = 0
            for matrix, first, place, width in window(group, 0, out.shape[1]):
                out[:, place : place + width] = columns(matrix, first, width, wide, down, embed)
                end = place + width
            if end < out.shape[1]:
                out[:, end:] = jnp.zeros((out.shape[0], out.shape[1] - end), out.dtype)


def sum_kernel(count, mom, *rest):
    received, g_out, y_out = rest[:count], rest[count], rest[count + 1]
    g = received[0][...].astype(jnp.float32)
    for piece in received[1:]:
        g = g + piece[...].astype(jnp.float32)
    g_out[...] = g.astype(jnp.bfloat16)
    y_out[...] = (g + MOMENTUM * (MOMENTUM * mom[...] + g)).astype(jnp.bfloat16)


def stack_kernel(count, *rest):
    out, rows = rest[-1], rest[0].shape[0]
    for number in range(count):
        out[number * rows : (number + 1) * rows, :] = rest[number][...]


def newton_kernel(bins, count, rows, index, *rest):
    pieces, out, x_ref = rest[:count], rest[-2], rest[-1]
    start = 0
    for piece in pieces:
        x_ref[start : start + piece.shape[0], :] = piece[...]
        start += piece.shape[0]

    def branch(group):
        spans = []
        offset = 0
        for matrix in group:
            end = offset + PADDED[matrix]
            tiles = [slice(low, min(low + TILE, end)) for low in range(offset, end, TILE)]
            spans.append((slice(offset, end), tiles, math.sqrt(max(D, WIDTHS[matrix]))))
            offset = end

        def outer(span):
            x = x_ref[:, span]
            return lax.dot_general(x, x, (((1,), (1,)), ((), ())), preferred_element_type=jnp.float32)

        def polynomial(gram):
            gram = gram.astype(jnp.bfloat16)
            square = jnp.dot(gram, gram, preferred_element_type=jnp.float32)
            return COEF_B * gram.astype(jnp.float32) + COEF_C * square

        def advance(tiles, poly, factor):
            for tile in tiles:
                x = x_ref[:, tile]
                x_ref[:, tile] = (
                    factor * x.astype(jnp.float32) + jnp.dot(poly, x, preferred_element_type=jnp.float32)
                ).astype(jnp.bfloat16)

        diagonal = lax.broadcasted_iota(jnp.int32, (D, D), 0) == lax.broadcasted_iota(jnp.int32, (D, D), 1)
        for span, tiles, _ in spans:
            gram = outer(span)
            scale = 1.0 / (jnp.sqrt(jnp.sum(jnp.where(diagonal, gram, 0.0))) + EPSILON)
            poly = (scale * polynomial(gram * scale * scale)).astype(jnp.bfloat16)
            advance(tiles, poly, COEF_A * scale)

        def step(_, carry):
            polys = [polynomial(outer(span)).astype(jnp.bfloat16) for span, _, _ in spans]
            for poly, (_, tiles, _) in zip(polys, spans):
                advance(tiles, poly, COEF_A)
            return carry

        lax.fori_loop(0, NS_ITERS - 2, step, 0)
        for span, tiles, factor in spans:
            poly = polynomial(outer(span))[:rows].astype(jnp.bfloat16)
            for tile in tiles:
                x = x_ref[:, tile]
                out[:, tile] = (
                    factor
                    * (COEF_A * x[:rows].astype(jnp.float32) + jnp.dot(poly, x, preferred_element_type=jnp.float32))
                ).astype(jnp.bfloat16)

    for target, group in enumerate(bins):
        if group:

            @pl.when(index[0] == target)
            def _():
                branch(group)


def placed(bins):
    where = {}
    for owner, group in enumerate(bins):
        offset = 0
        for matrix in group:
            where[matrix] = (owner, offset)
            offset += PADDED[matrix]
    return where


def per_index(bins, index, body):
    for mine in range(len(bins)):

        @pl.when(index[0] == mine)
        def _():
            body(mine)


def momentum_kernel(bins, index, wide, down, embed, *rest):
    n = len(bins)
    pieces, (new_wide, new_down, new_embed) = rest[:n], rest[n:]
    where = placed(bins)

    def body(mine):
        for matrix in range(6):
            owner, offset = where[matrix]
            g = pieces[mine ^ owner][:, offset : offset + PADDED[matrix]].astype(jnp.float32)
            if matrix == DOWN:
                new_down[...] = MOMENTUM * down[...] + g
            elif matrix == EMBED:
                new_embed[...] = MOMENTUM * embed[...] + g[:, :CLASSES]
            else:
                span = slice(OFFSETS[matrix], OFFSETS[matrix] + WIDTHS[matrix])
                new_wide[:, span] = MOMENTUM * wide[:, span] + g

    per_index(bins, index, body)


def update_kernel(bins, index, *rest):
    n = len(bins)
    pieces, (upd_wide, upd_down, upd_embed) = rest[:n], rest[n:]
    where = placed(bins)

    def body(mine):
        for matrix in range(6):
            owner, offset = where[matrix]
            value = pieces[mine ^ owner][:, offset : offset + PADDED[matrix]]
            if matrix == DOWN:
                upd_down[...] = value
            elif matrix == EMBED:
                upd_embed[...] = value[:, :CLASSES]
            else:
                upd_wide[:, OFFSETS[matrix] : OFFSETS[matrix] + WIDTHS[matrix]] = value

    per_index(bins, index, body)


VMEM = pl.BlockSpec(memory_space=pltpu.VMEM)
SMEM = pl.BlockSpec(memory_space=pltpu.SMEM)
ANY = pl.BlockSpec(memory_space=pl.ANY)


def call(kernel, outs, args, specs, scratch=(), flops=0, limit=VMEM_LIMIT):
    size = sum(a.size * a.dtype.itemsize for a in args) + sum(
        math.prod(o.shape) * o.dtype.itemsize for o in outs
    )
    return pl.pallas_call(
        kernel,
        out_shape=tuple(outs),
        in_specs=specs,
        out_specs=tuple([VMEM] * len(outs)),
        scratch_shapes=list(scratch),
        compiler_params=pltpu.CompilerParams(vmem_limit_bytes=limit),
        cost_estimate=pl.CostEstimate(flops=flops, bytes_accessed=size, transcendentals=0),
    )(*args)


def swap(value, axis, k, n):
    return lax.ppermute(value, axis, [(i, i ^ k) for i in range(n)])


def spread(value, axis, n):
    return [swap(value, axis, k, n) for k in range(1, n)]


def gather_rows(value, n):
    pieces = [value] + [swap(value, "shard", k, n) for k in range(2, n, 2)]
    rows, width = value.shape
    if rows % 16:
        pieces = [jnp.concatenate(pieces, axis=0)]
        return [jnp.concatenate(pieces + [swap(pieces[0], "shard", 1, n)], axis=0)]
    return pieces + [swap(piece, "shard", 1, n) for piece in pieces]


def per_device(grad_wide, grad_down, grad_embed, mom_wide, mom_down, mom_embed):
    n_rep, n_shard = lax.axis_size("rep"), lax.axis_size("shard")
    bins, width = plan(n_rep)
    index = lax.axis_index("rep").astype(jnp.int32).reshape(1)
    grads = (grad_wide[0, 0], grad_down[0, 0].T, grad_embed[0].T)
    moms = (mom_wide[0], mom_down[0].T, mom_embed.T)
    rows = grads[0].shape[0]
    whole = jax.ShapeDtypeStruct((rows, width), jnp.bfloat16)

    own, *sends = call(
        functools.partial(split_kernel, bins, [(0, width)]),
        [whole] * n_rep,
        (index, *grads),
        [SMEM] + [ANY] * 3,
        [pltpu.VMEM(array.shape, jnp.float32) for array in grads] + [pltpu.SemaphoreType.DMA((3,))],
        limit=VMEM_ALL,
    )
    received = [own] + [swap(piece, "rep", k + 1, n_rep) for k, piece in enumerate(sends)]
    (mom_own,) = call(
        functools.partial(own_kernel, bins),
        [jax.ShapeDtypeStruct((rows, width), jnp.float32)],
        (index, *moms),
        [SMEM] + [VMEM] * 3,
    )
    g, y = call(functools.partial(sum_kernel, n_rep), [whole] * 2, (mom_own, *received), [VMEM] * (n_rep + 1))
    pieces = gather_rows(y, n_shard)
    g_others = spread(g, "rep", n_rep)
    tied = g_others[: n_rep // 2]
    (upd,) = call(
        functools.partial(newton_kernel, bins, len(pieces), rows),
        [whole],
        (index, *pieces, *tied),
        [SMEM] + [VMEM] * len(pieces) + [ANY] * len(tied),
        (pltpu.VMEM((D, width), jnp.bfloat16),),
        flops=NS_ITERS * (4 * D * D * width + 2 * D * D * D),
    )
    upd_others = spread(upd, "rep", n_rep)
    news = call(
        functools.partial(momentum_kernel, bins),
        [jax.ShapeDtypeStruct(m.shape, jnp.float32) for m in moms],
        (index, *moms, g, *g_others),
        [SMEM] + [VMEM] * (3 + n_rep),
    )
    updates = call(
        functools.partial(update_kernel, bins),
        [jax.ShapeDtypeStruct(m.shape, jnp.bfloat16) for m in moms],
        (index, upd, *upd_others),
        [SMEM] + [VMEM] * n_rep,
    )
    return (
        news[0][None],
        news[1].T[None],
        news[2].T,
        updates[0][None],
        updates[1].T[None],
        updates[2].T,
    )


def solution(mesh):
    placed_in = (
        P("rep", None, "shard", None),
        P("rep", None, None, "shard"),
        P("rep", None, "shard"),
        P(None, "shard", None),
        P(None, None, "shard"),
        P(None, "shard"),
    )
    return jax.shard_map(
        per_device,
        mesh=mesh,
        in_specs=placed_in,
        out_specs=placed_in[3:] + placed_in[3:],
        check_vma=False,
    )
```

```python
import functools
import math

import jax
import jax.numpy as jnp
from jax import lax
from jax.experimental import pallas as pl
from jax.experimental.pallas import tpu as pltpu
from jax.sharding import PartitionSpec as P

D = 384
MLP = 1536
ADA = 2304
CLASSES = 1001
NS_ITERS = 5
QKV = 1152

COEF_A = 3.4445
COEF_B = -4.775
COEF_C = 2.0315
MOMENTUM = 0.95
EPSILON = 1e-07

VMEM_LIMIT = 48 * 1024 * 1024
VMEM_ALL = 63 * 1024 * 1024

WIDTHS = [QKV, D, MLP, ADA, MLP, CLASSES]
OFFSETS = [0, QKV, QKV + D, QKV + D + MLP]
PADDED = [-(-width // 128) * 128 for width in WIDTHS]
DOWN, EMBED = 4, 5
TILE = 256


def plan(n_rep):
    bins = [[] for _ in range(n_rep)]
    loads = [0] * n_rep
    for matrix in sorted(range(6), key=lambda m: -PADDED[m]):
        owner = loads.index(min(loads))
        bins[owner].append(matrix)
        loads[owner] += PADDED[matrix]
    return bins, max(loads)


def window(group, low, high):
    found = []
    offset = 0
    for matrix in group:
        first, last = max(low - offset, 0), min(high - offset, PADDED[matrix])
        if first < last:
            found.append((matrix, first, offset + first - low, last - first))
        offset += PADDED[matrix]
    return found


def columns(matrix, first, width, wide, down, embed):
    if matrix == DOWN:
        return down[:, first : first + width]
    if matrix == EMBED:
        last = min(first + width, CLASSES)
        value = embed[:, first:last]
        if last < first + width:
            tail = jnp.zeros((value.shape[0], first + width - last), value.dtype)
            value = jnp.concatenate([value, tail], axis=1)
        return value
    return wide[:, OFFSETS[matrix] + first : OFFSETS[matrix] + first + width]


def split_kernel(bins, windows, index, wide, down, embed, *rest):
    n = len(bins)
    outs, held, sems = rest[: len(windows) * n], rest[-4:-1], rest[-1]
    copies = [pltpu.make_async_copy(src, dst, sems.at[i]) for i, (src, dst) in enumerate(zip((wide, down, embed), held))]
    for copy in copies:
        copy.start()
    for copy in copies:
        copy.wait()
    for half, (low, high) in enumerate(windows):
        for k in range(n):
            dst = outs[half * n + k]
            for target, group in enumerate(bins):

                @pl.when((index[0] ^ k) == target)
                def _():
                    end = 0
                    for matrix, first, place, width in window(group, low, high):
                        dst[:, place : place + width] = columns(matrix, first, width, *held).astype(dst.dtype)
                        end = place + width
                    if end < high - low:
                        dst[:, end:] = jnp.zeros((dst.shape[0], high - low - end), dst.dtype)


def own_kernel(bins, windows, index, wide, down, embed, *outs):
    for target, group in enumerate(bins):

        @pl.when(index[0] == target)
        def _():
            for out, (low, high) in zip(outs, windows):
                end = 0
                for matrix, first, place, width in window(group, low, high):
                    out[:, place : place + width] = columns(matrix, first, width, wide, down, embed)
                    end = place + width
                if end < high - low:
                    out[:, end:] = jnp.zeros((out.shape[0], high - low - end), out.dtype)


def sum_kernel(count, mom, *rest):
    received, g_out, y_out = rest[:count], rest[-2], rest[-1]
    g = received[0][...].astype(jnp.float32)
    for piece in received[1:]:
        g = g + piece[...].astype(jnp.float32)
    g_out[...] = g.astype(jnp.bfloat16)
    y_out[...] = (g + MOMENTUM * (MOMENTUM * mom[...] + g)).astype(jnp.bfloat16)


def join_kernel(left, right, *rest):
    out, half = rest[-1], left.shape[1]
    out[:, :half] = left[...]
    out[:, half:] = right[...]


def stack_kernel(count, *rest):
    out, rows = rest[-1], rest[0].shape[0]
    for number in range(count):
        out[number * rows : (number + 1) * rows, :] = rest[number][...]


def newton_kernel(bins, halves, count, index, *rest):
    out, x_ref = rest[-2], rest[-1]
    left = 0
    for half in range(halves):
        pieces = rest[half * count : (half + 1) * count]
        top = 0
        for piece in pieces:
            x_ref[top : top + piece.shape[0], left : left + piece.shape[1]] = piece[...]
            top += piece.shape[0]
        left += pieces[0].shape[1]
    rows = out.shape[0]

    def branch(group):
        spans = []
        offset = 0
        for matrix in group:
            end = offset + PADDED[matrix]
            tiles = [slice(low, min(low + TILE, end)) for low in range(offset, end, TILE)]
            spans.append((slice(offset, end), tiles, math.sqrt(max(D, WIDTHS[matrix]))))
            offset = end

        def outer(span):
            x = x_ref[:, span]
            return lax.dot_general(x, x, (((1,), (1,)), ((), ())), preferred_element_type=jnp.float32)

        def polynomial(gram):
            gram = gram.astype(jnp.bfloat16)
            square = jnp.dot(gram, gram, preferred_element_type=jnp.float32)
            return COEF_B * gram.astype(jnp.float32) + COEF_C * square

        def advance(tiles, poly, factor):
            for tile in tiles:
                x = x_ref[:, tile]
                x_ref[:, tile] = (
                    factor * x.astype(jnp.float32) + jnp.dot(poly, x, preferred_element_type=jnp.float32)
                ).astype(jnp.bfloat16)

        diagonal = lax.broadcasted_iota(jnp.int32, (D, D), 0) == lax.broadcasted_iota(jnp.int32, (D, D), 1)
        for span, tiles, _ in spans:
            gram = outer(span)
            scale = 1.0 / (jnp.sqrt(jnp.sum(jnp.where(diagonal, gram, 0.0))) + EPSILON)
            poly = (scale * polynomial(gram * scale * scale)).astype(jnp.bfloat16)
            advance(tiles, poly, COEF_A * scale)

        def step(_, carry):
            polys = [polynomial(outer(span)).astype(jnp.bfloat16) for span, _, _ in spans]
            for poly, (_, tiles, _) in zip(polys, spans):
                advance(tiles, poly, COEF_A)
            return carry

        lax.fori_loop(0, NS_ITERS - 2, step, 0)
        for span, tiles, factor in spans:
            poly = polynomial(outer(span))[:rows].astype(jnp.bfloat16)
            for tile in tiles:
                x = x_ref[:, tile]
                out[:, tile] = (
                    factor
                    * (COEF_A * x[:rows].astype(jnp.float32) + jnp.dot(poly, x, preferred_element_type=jnp.float32))
                ).astype(jnp.bfloat16)

    for target, group in enumerate(bins):
        if group:

            @pl.when(index[0] == target)
            def _():
                branch(group)


def placed(bins):
    where = {}
    for owner, group in enumerate(bins):
        offset = 0
        for matrix in group:
            where[matrix] = (owner, offset)
            offset += PADDED[matrix]
    return where


def per_index(bins, index, body):
    for mine in range(len(bins)):

        @pl.when(index[0] == mine)
        def _():
            body(mine)


def momentum_kernel(bins, index, wide, down, embed, *rest):
    n = len(bins)
    pieces, (new_wide, new_down, new_embed) = rest[:n], rest[n:]
    where = placed(bins)

    def body(mine):
        for matrix in range(6):
            owner, offset = where[matrix]
            g = pieces[mine ^ owner][:, offset : offset + PADDED[matrix]].astype(jnp.float32)
            if matrix == DOWN:
                new_down[...] = MOMENTUM * down[...] + g
            elif matrix == EMBED:
                new_embed[...] = MOMENTUM * embed[...] + g[:, :CLASSES]
            else:
                span = slice(OFFSETS[matrix], OFFSETS[matrix] + WIDTHS[matrix])
                new_wide[:, span] = MOMENTUM * wide[:, span] + g

    per_index(bins, index, body)


def update_kernel(bins, index, *rest):
    n = len(bins)
    pieces, (upd_wide, upd_down, upd_embed) = rest[:n], rest[n:]
    where = placed(bins)

    def body(mine):
        for matrix in range(6):
            owner, offset = where[matrix]
            value = pieces[mine ^ owner][:, offset : offset + PADDED[matrix]]
            if matrix == DOWN:
                upd_down[...] = value
            elif matrix == EMBED:
                upd_embed[...] = value[:, :CLASSES]
            else:
                upd_wide[:, OFFSETS[matrix] : OFFSETS[matrix] + WIDTHS[matrix]] = value

    per_index(bins, index, body)


VMEM = pl.BlockSpec(memory_space=pltpu.VMEM)
SMEM = pl.BlockSpec(memory_space=pltpu.SMEM)
ANY = pl.BlockSpec(memory_space=pl.ANY)


def call(kernel, outs, args, specs, scratch=(), flops=0, limit=VMEM_LIMIT):
    size = sum(a.size * a.dtype.itemsize for a in args) + sum(
        math.prod(o.shape) * o.dtype.itemsize for o in outs
    )
    return pl.pallas_call(
        kernel,
        out_shape=tuple(outs),
        in_specs=specs,
        out_specs=tuple([VMEM] * len(outs)),
        scratch_shapes=list(scratch),
        compiler_params=pltpu.CompilerParams(vmem_limit_bytes=limit),
        cost_estimate=pl.CostEstimate(flops=flops, bytes_accessed=size, transcendentals=0),
    )(*args)


def swap(value, axis, k, n):
    return lax.ppermute(value, axis, [(i, i ^ k) for i in range(n)])


def spread(value, axis, n):
    return [swap(value, axis, k, n) for k in range(1, n)]


def stack(pieces, tied=()):
    rows, width = pieces[0].shape
    if rows % 16:
        return jnp.concatenate(pieces, axis=0)
    return call(
        functools.partial(stack_kernel, len(pieces)),
        [jax.ShapeDtypeStruct((rows * len(pieces), width), pieces[0].dtype)],
        (*pieces, *tied),
        [VMEM] * len(pieces) + [ANY] * len(tied),
    )[0]


def per_device(grad_wide, grad_down, grad_embed, mom_wide, mom_down, mom_embed):
    n_rep, n_shard = lax.axis_size("rep"), lax.axis_size("shard")
    bins, width = plan(n_rep)
    index = lax.axis_index("rep").astype(jnp.int32).reshape(1)
    grads = (grad_wide[0, 0], grad_down[0, 0].T, grad_embed[0].T)
    moms = (mom_wide[0], mom_down[0].T, mom_embed.T)
    rows = grads[0].shape[0]
    windows = [(0, width // 2), (width // 2, width)]

    def block(columns, dtype=jnp.bfloat16):
        return jax.ShapeDtypeStruct((rows, columns), dtype)

    sends = call(
        functools.partial(split_kernel, bins, windows),
        [block(high - low) for low, high in windows for _ in range(n_rep)],
        (index, *grads),
        [SMEM] + [ANY] * 3,
        [pltpu.VMEM(array.shape, jnp.float32) for array in grads] + [pltpu.SemaphoreType.DMA((3,))],
        limit=VMEM_ALL,
    )
    mom_own = call(
        functools.partial(own_kernel, bins, windows),
        [block(high - low, jnp.float32) for low, high in windows],
        (index, *moms),
        [SMEM] + [VMEM] * 3,
    )
    gs, arrived = [], []
    for half, (low, high) in enumerate(windows):
        own, *others = sends[half * n_rep : (half + 1) * n_rep]
        received = [own] + [swap(piece, "rep", k + 1, n_rep) for k, piece in enumerate(others)]
        g, y = call(
            functools.partial(sum_kernel, n_rep),
            [block(high - low)] * 2,
            (mom_own[half], *received),
            [VMEM] * (n_rep + 1),
        )
        gs.append(g)
        arrived.append([y] + [swap(y, "shard", k, n_shard) for k in range(2, n_shard, 2)])
    stacks = [None, stack(arrived[1], (arrived[0][0],))]
    (g,) = call(join_kernel, [block(width)], (*gs, arrived[1][1]), [VMEM] * 2 + [ANY])
    g_others = spread(g, "rep", n_rep)
    stacks[0] = stack(arrived[0], g_others[:2])
    pieces = [piece for whole in stacks for piece in (whole, swap(whole, "shard", 1, n_shard))]
    (upd,) = call(
        functools.partial(newton_kernel, bins, 2, 2),
        [block(width)],
        (index, *pieces),
        [SMEM] + [VMEM] * len(pieces),
        (pltpu.VMEM((D, width), jnp.bfloat16),),
        flops=NS_ITERS * (4 * D * D * width + 2 * D * D * D),
    )
    upd_others = spread(upd, "rep", n_rep)
    news = call(
        functools.partial(momentum_kernel, bins),
        [jax.ShapeDtypeStruct(m.shape, jnp.float32) for m in moms],
        (index, *moms, g, *g_others),
        [SMEM] + [VMEM] * (3 + n_rep),
    )
    updates = call(
        functools.partial(update_kernel, bins),
        [jax.ShapeDtypeStruct(m.shape, jnp.bfloat16) for m in moms],
        (index, upd, *upd_others),
        [SMEM] + [VMEM] * n_rep,
    )
    return (
        news[0][None],
        news[1].T[None],
        news[2].T,
        updates[0][None],
        updates[1].T[None],
        updates[2].T,
    )


def solution(mesh):
    placed_in = (
        P("rep", None, "shard", None),
        P("rep", None, None, "shard"),
        P("rep", None, "shard"),
        P(None, "shard", None),
        P(None, None, "shard"),
        P(None, "shard"),
    )
    return jax.shard_map(
        per_device,
        mesh=mesh,
        in_specs=placed_in,
        out_specs=placed_in[3:] + placed_in[3:],
        check_vma=False,
    )
```

```python
import functools
import math

import jax
import jax.numpy as jnp
from jax import lax
from jax.experimental import pallas as pl
from jax.experimental.pallas import tpu as pltpu
from jax.sharding import PartitionSpec as P

D = 384
MLP = 1536
ADA = 2304
CLASSES = 1001
NS_ITERS = 5
QKV = 1152

COEF_A = 3.4445
COEF_B = -4.775
COEF_C = 2.0315
MOMENTUM = 0.95
EPSILON = 1e-07

FORWARD = (True, True)
VMEM_LIMIT = 48 * 1024 * 1024
VMEM_ALL = 62 * 1024 * 1024

WIDTHS = [QKV, D, MLP, ADA, MLP, CLASSES]
OFFSETS = [0, QKV, QKV + D, QKV + D + MLP]
PADDED = [-(-width // 128) * 128 for width in WIDTHS]
DOWN, EMBED = 4, 5
TILE = 256


def plan(n_rep):
    bins = [[] for _ in range(n_rep)]
    loads = [0] * n_rep
    for matrix in sorted(range(6), key=lambda m: -PADDED[m]):
        owner = loads.index(min(loads))
        bins[owner].append(matrix)
        loads[owner] += PADDED[matrix]
    return bins, max(loads)


def window(group, low, high):
    found = []
    offset = 0
    for matrix in group:
        first, last = max(low - offset, 0), min(high - offset, PADDED[matrix])
        if first < last:
            found.append((matrix, first, offset + first - low, last - first))
        offset += PADDED[matrix]
    return found


def columns(matrix, first, width, wide, down, embed):
    if matrix == DOWN:
        return down[:, first : first + width]
    if matrix == EMBED:
        last = min(first + width, CLASSES)
        value = embed[:, first:last]
        if last < first + width:
            tail = jnp.zeros((value.shape[0], first + width - last), value.dtype)
            value = jnp.concatenate([value, tail], axis=1)
        return value
    return wide[:, OFFSETS[matrix] + first : OFFSETS[matrix] + first + width]


def split_kernel(bins, windows, index, wide, down, embed, *rest):
    n = len(bins)
    outs, held, sems = rest[: len(windows) * n], rest[-4:-1], rest[-1]
    copies = [pltpu.make_async_copy(src, dst, sems.at[i]) for i, (src, dst) in enumerate(zip((wide, down, embed), held))]
    for copy in copies:
        copy.start()
    for copy in copies:
        copy.wait()
    for half, (low, high) in enumerate(windows):
        for k in range(n):
            dst = outs[half * n + k]
            for target, group in enumerate(bins):

                @pl.when((index[0] ^ k) == target)
                def _():
                    end = 0
                    for matrix, first, place, width in window(group, low, high):
                        dst[:, place : place + width] = columns(matrix, first, width, *held).astype(dst.dtype)
                        end = place + width
                    if end < high - low:
                        dst[:, end:] = jnp.zeros((dst.shape[0], high - low - end), dst.dtype)


def own_kernel(bins, windows, index, wide, down, embed, *outs):
    for target, group in enumerate(bins):

        @pl.when(index[0] == target)
        def _():
            for out, (low, high) in zip(outs, windows):
                end = 0
                for matrix, first, place, width in window(group, low, high):
                    out[:, place : place + width] = columns(matrix, first, width, wide, down, embed)
                    end = place + width
                if end < high - low:
                    out[:, end:] = jnp.zeros((out.shape[0], high - low - end), out.dtype)


def sum_kernel(count, mom, *rest):
    received, g_out, y_out = rest[:count], rest[-2], rest[-1]
    g = received[0][...].astype(jnp.float32)
    for piece in received[1:]:
        g = g + piece[...].astype(jnp.float32)
    g_out[...] = g.astype(jnp.bfloat16)
    y_out[...] = (g + MOMENTUM * (MOMENTUM * mom[...] + g)).astype(jnp.bfloat16)


def join_kernel(left, right, *rest):
    out, half = rest[-1], left.shape[1]
    out[:, :half] = left[...]
    out[:, half:] = right[...]


def stack_kernel(blocks, *rest):
    out, rows = rest[-1], rest[0].shape[0]
    for number, (first, *others) in enumerate(blocks):
        value = rest[first][...]
        for extra in others:
            value = value + rest[extra][...]
        out[number * rows : (number + 1) * rows, :] = value


def newton_kernel(bins, halves, count, index, *rest):
    out, x_ref = rest[-2], rest[-1]
    left = 0
    for half in range(halves):
        pieces = rest[half * count : (half + 1) * count]
        top = 0
        for piece in pieces:
            x_ref[top : top + piece.shape[0], left : left + piece.shape[1]] = piece[...]
            top += piece.shape[0]
        left += pieces[0].shape[1]
    rows = out.shape[0]

    def branch(group):
        spans = []
        offset = 0
        for matrix in group:
            end = offset + PADDED[matrix]
            tiles = [slice(low, min(low + TILE, end)) for low in range(offset, end, TILE)]
            spans.append((slice(offset, end), tiles, math.sqrt(max(D, WIDTHS[matrix]))))
            offset = end

        def outer(span):
            x = x_ref[:, span]
            return lax.dot_general(x, x, (((1,), (1,)), ((), ())), preferred_element_type=jnp.float32)

        def polynomial(gram):
            gram = gram.astype(jnp.bfloat16)
            square = jnp.dot(gram, gram, preferred_element_type=jnp.float32)
            return COEF_B * gram.astype(jnp.float32) + COEF_C * square

        def advance(tiles, poly, factor):
            for tile in tiles:
                x = x_ref[:, tile]
                x_ref[:, tile] = (
                    factor * x.astype(jnp.float32) + jnp.dot(poly, x, preferred_element_type=jnp.float32)
                ).astype(jnp.bfloat16)

        diagonal = lax.broadcasted_iota(jnp.int32, (D, D), 0) == lax.broadcasted_iota(jnp.int32, (D, D), 1)
        for span, tiles, _ in spans:
            gram = outer(span)
            scale = 1.0 / (jnp.sqrt(jnp.sum(jnp.where(diagonal, gram, 0.0))) + EPSILON)
            poly = (scale * polynomial(gram * scale * scale)).astype(jnp.bfloat16)
            advance(tiles, poly, COEF_A * scale)

        def step(_, carry):
            polys = [polynomial(outer(span)).astype(jnp.bfloat16) for span, _, _ in spans]
            for poly, (_, tiles, _) in zip(polys, spans):
                advance(tiles, poly, COEF_A)
            return carry

        lax.fori_loop(0, NS_ITERS - 2, step, 0)
        for span, tiles, factor in spans:
            poly = polynomial(outer(span))[:rows].astype(jnp.bfloat16)
            for tile in tiles:
                x = x_ref[:, tile]
                out[:, tile] = (
                    factor
                    * (COEF_A * x[:rows].astype(jnp.float32) + jnp.dot(poly, x, preferred_element_type=jnp.float32))
                ).astype(jnp.bfloat16)

    for target, group in enumerate(bins):
        if group:

            @pl.when(index[0] == target)
            def _():
                branch(group)


def placed(bins):
    where = {}
    for owner, group in enumerate(bins):
        offset = 0
        for matrix in group:
            where[matrix] = (owner, offset)
            offset += PADDED[matrix]
    return where


def per_index(bins, index, body):
    for mine in range(len(bins)):

        @pl.when(index[0] == mine)
        def _():
            body(mine)


def momentum_kernel(bins, index, wide, down, embed, *rest):
    pieces, (new_wide, new_down, new_embed) = rest[:-3], rest[-3:]
    where = placed(bins)
    rows = wide.shape[0]
    each = pieces[0].shape[0] // rows

    def body(mine):
        for matrix in range(6):
            owner, offset = where[matrix]
            number, place = divmod(mine ^ owner, each)
            block = pieces[number][place * rows : (place + 1) * rows, offset : offset + PADDED[matrix]]
            g = block.astype(jnp.float32)
            if matrix == DOWN:
                new_down[...] = MOMENTUM * down[...] + g
            elif matrix == EMBED:
                new_embed[...] = MOMENTUM * embed[...] + g[:, :CLASSES]
            else:
                span = slice(OFFSETS[matrix], OFFSETS[matrix] + WIDTHS[matrix])
                new_wide[:, span] = MOMENTUM * wide[:, span] + g

    per_index(bins, index, body)


def update_kernel(bins, index, *rest):
    n = len(bins)
    pieces, (upd_wide, upd_down, upd_embed) = rest[:n], rest[n:]
    where = placed(bins)

    def body(mine):
        for matrix in range(6):
            owner, offset = where[matrix]
            value = pieces[mine ^ owner][:, offset : offset + PADDED[matrix]]
            if matrix == DOWN:
                upd_down[...] = value
            elif matrix == EMBED:
                upd_embed[...] = value[:, :CLASSES]
            else:
                upd_wide[:, OFFSETS[matrix] : OFFSETS[matrix] + WIDTHS[matrix]] = value

    per_index(bins, index, body)


VMEM = pl.BlockSpec(memory_space=pltpu.VMEM)
SMEM = pl.BlockSpec(memory_space=pltpu.SMEM)
ANY = pl.BlockSpec(memory_space=pl.ANY)


def call(kernel, outs, args, specs, scratch=(), flops=0, limit=VMEM_LIMIT):
    size = sum(a.size * a.dtype.itemsize for a in args) + sum(
        math.prod(o.shape) * o.dtype.itemsize for o in outs
    )
    return pl.pallas_call(
        kernel,
        out_shape=tuple(outs),
        in_specs=specs,
        out_specs=tuple([VMEM] * len(outs)),
        scratch_shapes=list(scratch),
        compiler_params=pltpu.CompilerParams(vmem_limit_bytes=limit),
        cost_estimate=pl.CostEstimate(flops=flops, bytes_accessed=size, transcendentals=0),
    )(*args)


def swap(value, axis, k, n):
    return lax.ppermute(value, axis, [(i, i ^ k) for i in range(n)])


def spread(value, axis, n):
    return [swap(value, axis, k, n) for k in range(1, n)]


def stack(pieces, tied=(), blocks=None):
    rows, width = pieces[0].shape
    blocks = blocks or [[number] for number in range(len(pieces))]
    if rows % 16:
        return jnp.concatenate([sum(pieces[i] for i in block) for block in blocks], axis=0)
    return call(
        functools.partial(stack_kernel, blocks),
        [jax.ShapeDtypeStruct((rows * len(blocks), width), pieces[0].dtype)],
        (*pieces, *tied),
        [VMEM] * len(pieces) + [ANY] * len(tied),
    )[0]


def along(value, hops):
    return lax.ppermute(value, "shard", [(2 * a + c, 2 * b + c) for a, b in hops for c in range(2)])


def cross(value, n, forward):
    if n == 8 and forward:
        far = along(value, [(0, 2), (2, 0), (1, 3), (3, 1)])
        near = along(value, [(0, 1), (1, 0), (2, 3), (3, 2)])
        middle = along(value, [(1, 2), (2, 1)])
        ends = along(far, [(2, 3), (1, 0)])
        return [value, near, far, middle, ends], [[0], [1], [2], [3, 4]]
    pieces = [value] + [swap(value, "shard", k, n) for k in range(2, n, 2)]
    return pieces, [[number] for number in range(len(pieces))]


def per_device(grad_wide, grad_down, grad_embed, mom_wide, mom_down, mom_embed):
    n_rep, n_shard = lax.axis_size("rep"), lax.axis_size("shard")
    bins, width = plan(n_rep)
    index = lax.axis_index("rep").astype(jnp.int32).reshape(1)
    grads = (grad_wide[0, 0], grad_down[0, 0].T, grad_embed[0].T)
    moms = (mom_wide[0], mom_down[0].T, mom_embed.T)
    rows = grads[0].shape[0]
    windows = [(0, width // 2), (width // 2, width)]

    def block(columns, dtype=jnp.bfloat16):
        return jax.ShapeDtypeStruct((rows, columns), dtype)

    sends = call(
        functools.partial(split_kernel, bins, windows),
        [block(high - low) for low, high in windows for _ in range(n_rep)],
        (index, *grads),
        [SMEM] + [ANY] * 3,
        [pltpu.VMEM(array.shape, jnp.float32) for array in grads] + [pltpu.SemaphoreType.DMA((3,))],
        limit=VMEM_ALL,
    )
    mom_own = call(
        functools.partial(own_kernel, bins, windows),
        [block(high - low, jnp.float32) for low, high in windows],
        (index, *moms),
        [SMEM] + [VMEM] * 3,
    )
    gs, arrived, blocks = [], [], []
    for half, (low, high) in enumerate(windows):
        own, *others = sends[half * n_rep : (half + 1) * n_rep]
        received = [own] + [swap(piece, "rep", k + 1, n_rep) for k, piece in enumerate(others)]
        g, y = call(
            functools.partial(sum_kernel, n_rep),
            [block(high - low)] * 2,
            (mom_own[half], *received),
            [VMEM] * (n_rep + 1),
        )
        gs.append(g)
        crossed = cross(y, n_shard, FORWARD[half])
        arrived.append(crossed[0])
        blocks.append(crossed[1])
    stacks = [None, stack(arrived[1], (arrived[0][0],), blocks[1])]
    (g,) = call(join_kernel, [block(width)], (*gs, arrived[1][1]), [VMEM] * 2 + [ANY])
    g_first = swap(g, "rep", 1, n_rep)
    g_pair = [g, g_first]
    if n_rep == 4 and rows % 16 == 0:
        twice = stack(g_pair)
        g_all = [twice, swap(twice, "rep", 2, n_rep)]
    else:
        g_all = g_pair + spread(g, "rep", n_rep)[1:]
    stacks[0] = stack(arrived[0], (g_first,), blocks[0])
    pieces = [piece for whole in stacks for piece in (whole, swap(whole, "shard", 1, n_shard))]
    (upd,) = call(
        functools.partial(newton_kernel, bins, 2, 2),
        [block(width)],
        (index, *pieces, g_all[-1]),
        [SMEM] + [VMEM] * len(pieces) + [ANY],
        (pltpu.VMEM((D, width), jnp.bfloat16),),
        flops=NS_ITERS * (4 * D * D * width + 2 * D * D * D),
    )
    upd_others = spread(upd, "rep", n_rep)
    news = call(
        functools.partial(momentum_kernel, bins),
        [jax.ShapeDtypeStruct(m.shape, jnp.float32) for m in moms],
        (index, *moms, *g_all),
        [SMEM] + [VMEM] * (3 + len(g_all)),
    )
    updates = call(
        functools.partial(update_kernel, bins),
        [jax.ShapeDtypeStruct(m.shape, jnp.bfloat16) for m in moms],
        (index, upd, *upd_others),
        [SMEM] + [VMEM] * n_rep,
    )
    return (
        news[0][None],
        news[1].T[None],
        news[2].T,
        updates[0][None],
        updates[1].T[None],
        updates[2].T,
    )


def solution(mesh):
    placed_in = (
        P("rep", None, "shard", None),
        P("rep", None, None, "shard"),
        P("rep", None, "shard"),
        P(None, "shard", None),
        P(None, None, "shard"),
        P(None, "shard"),
    )
    return jax.shard_map(
        per_device,
        mesh=mesh,
        in_specs=placed_in,
        out_specs=placed_in[3:] + placed_in[3:],
        check_vma=False,
    )
```

```python
import functools
import math

import jax
import jax.numpy as jnp
from jax import lax
from jax.experimental import pallas as pl
from jax.experimental.pallas import tpu as pltpu
from jax.sharding import PartitionSpec as P

D = 384
MLP = 1536
ADA = 2304
CLASSES = 1001
NS_ITERS = 5
QKV = 1152

COEF_A = 3.4445
COEF_B = -4.775
COEF_C = 2.0315
MOMENTUM = 0.95
EPSILON = 1e-07

VMEM_LIMIT = 48 * 1024 * 1024
VMEM_ALL = 62 * 1024 * 1024

WIDTHS = [QKV, D, MLP, ADA, MLP, CLASSES]
OFFSETS = [0, QKV, QKV + D, QKV + D + MLP]
PADDED = [-(-width // 128) * 128 for width in WIDTHS]
DOWN, EMBED = 4, 5
TILE = 256
SPLIT = 256


def plan(n_rep):
    bins = [[] for _ in range(n_rep)]
    loads = [0] * n_rep
    for matrix in sorted(range(6), key=lambda m: -PADDED[m]):
        owner = loads.index(min(loads))
        bins[owner].append(matrix)
        loads[owner] += PADDED[matrix]
    return bins, max(loads)


def window(group, low, high):
    found = []
    offset = 0
    for matrix in group:
        first, last = max(low - offset, 0), min(high - offset, PADDED[matrix])
        if first < last:
            found.append((matrix, first, offset + first - low, last - first))
        offset += PADDED[matrix]
    return found


def columns(matrix, first, width, wide, down, embed):
    if matrix == DOWN:
        return down[:, first : first + width]
    if matrix == EMBED:
        last = min(first + width, CLASSES)
        value = embed[:, first:last]
        if last < first + width:
            tail = jnp.zeros((value.shape[0], first + width - last), value.dtype)
            value = jnp.concatenate([value, tail], axis=1)
        return value
    return wide[:, OFFSETS[matrix] + first : OFFSETS[matrix] + first + width]


def split_kernel(bins, windows, index, wide, down, embed, *rest):
    n = len(bins)
    outs, held, sems = rest[: len(windows) * n], rest[-4:-1], rest[-1]
    copies = [pltpu.make_async_copy(src, dst, sems.at[i]) for i, (src, dst) in enumerate(zip((wide, down, embed), held))]
    for copy in copies:
        copy.start()
    for copy in copies:
        copy.wait()
    for half, (low, high) in enumerate(windows):
        for k in range(n):
            dst = outs[half * n + k]
            for target, group in enumerate(bins):

                @pl.when((index[0] ^ k) == target)
                def _():
                    end = 0
                    for matrix, first, place, width in window(group, low, high):
                        dst[:, place : place + width] = columns(matrix, first, width, *held).astype(dst.dtype)
                        end = place + width
                    if end < high - low:
                        dst[:, end:] = jnp.zeros((dst.shape[0], high - low - end), dst.dtype)


def own_kernel(bins, windows, index, wide, down, embed, *outs):
    for target, group in enumerate(bins):

        @pl.when(index[0] == target)
        def _():
            for out, (low, high) in zip(outs, windows):
                end = 0
                for matrix, first, place, width in window(group, low, high):
                    out[:, place : place + width] = columns(matrix, first, width, wide, down, embed)
                    end = place + width
                if end < high - low:
                    out[:, end:] = jnp.zeros((out.shape[0], high - low - end), out.dtype)


def sum_kernel(count, mom, *rest):
    received, g_out, y_out = rest[:count], rest[-2], rest[-1]
    g = received[0][...].astype(jnp.float32)
    for piece in received[1:]:
        g = g + piece[...].astype(jnp.float32)
    g_out[...] = g.astype(jnp.bfloat16)
    y_out[...] = (g + MOMENTUM * (MOMENTUM * mom[...] + g)).astype(jnp.bfloat16)


def join_kernel(left, right, *rest):
    out, half = rest[-1], left.shape[1]
    out[:, :half] = left[...]
    out[:, half:] = right[...]


def stack_kernel(count, *rest):
    out, rows = rest[-1], rest[0].shape[0]
    for number in range(count):
        out[number * rows : (number + 1) * rows, :] = rest[number][...]


def newton_kernel(bins, halves, count, index, *rest):
    out, x_ref = rest[-2], rest[-1]
    left = 0
    for half in range(halves):
        pieces = rest[half * count : (half + 1) * count]
        top = 0
        for piece in pieces:
            x_ref[top : top + piece.shape[0], left : left + piece.shape[1]] = piece[...]
            top += piece.shape[0]
        left += pieces[0].shape[1]
    rows = out.shape[0]

    def branch(group):
        spans = []
        offset = 0
        for matrix in group:
            end = offset + PADDED[matrix]
            tiles = [slice(low, min(low + TILE, end)) for low in range(offset, end, TILE)]
            spans.append((slice(offset, end), tiles, math.sqrt(max(D, WIDTHS[matrix]))))
            offset = end

        def product(left, right, sides):
            return lax.dot_general(left, right, ((sides[0], sides[1]), ((), ())), preferred_element_type=jnp.float32)

        def symmetric(left, corner):
            right = jnp.concatenate([left[SPLIT:, :].T, corner], axis=0)
            return jnp.concatenate([left, right], axis=1)

        def outer(span):
            sides = ((1,), (1,))
            left = product(x_ref[:, span], x_ref[:SPLIT, span], sides)
            low = x_ref[SPLIT:, span]
            return symmetric(left, product(low, low, sides))

        def polynomial(gram, scale=1.0):
            gram = gram.astype(jnp.bfloat16)
            sides = ((1,), (0,))

            def entries(value, square, diagonal):
                value = COEF_B * value.astype(jnp.float32) + COEF_C * square
                return scale * (value + jnp.where(diagonal, COEF_A, 0.0))

            left = entries(gram[:, :SPLIT], product(gram, gram[:, :SPLIT], sides), diagonal[:, :SPLIT])
            corner = product(gram[SPLIT:, :], gram[:, SPLIT:], sides)
            corner = entries(gram[SPLIT:, SPLIT:], corner, diagonal[SPLIT:, SPLIT:])
            return symmetric(left, corner).astype(jnp.bfloat16)

        def advance(tiles, poly):
            for tile in tiles:
                x_ref[:, tile] = product(poly, x_ref[:, tile], ((1,), (0,))).astype(jnp.bfloat16)

        row = lax.broadcasted_iota(jnp.int32, (D, D), 0)
        diagonal = row == lax.broadcasted_iota(jnp.int32, (D, D), 1)
        for span, tiles, _ in spans:
            gram = outer(span)
            scale = 1.0 / (jnp.sqrt(jnp.sum(jnp.where(diagonal, gram, 0.0))) + EPSILON)
            advance(tiles, polynomial(gram * scale * scale, scale))

        def step(_, carry):
            polys = [polynomial(outer(span)) for span, _, _ in spans]
            for poly, (_, tiles, _) in zip(polys, spans):
                advance(tiles, poly)
            return carry

        lax.fori_loop(0, NS_ITERS - 2, step, 0)
        for span, tiles, factor in spans:
            poly = polynomial(outer(span))[:rows]
            for tile in tiles:
                value = product(poly, x_ref[:, tile], ((1,), (0,)))
                out[:, tile] = (factor * value).astype(jnp.bfloat16)

    for target, group in enumerate(bins):
        if group:

            @pl.when(index[0] == target)
            def _():
                branch(group)


def placed(bins):
    where = {}
    for owner, group in enumerate(bins):
        offset = 0
        for matrix in group:
            where[matrix] = (owner, offset)
            offset += PADDED[matrix]
    return where


def per_index(bins, index, body):
    for mine in range(len(bins)):

        @pl.when(index[0] == mine)
        def _():
            body(mine)


def momentum_kernel(bins, index, wide, down, embed, *rest):
    n = len(bins)
    pieces, (new_wide, new_down, new_embed) = rest[:n], rest[n:]
    where = placed(bins)

    def body(mine):
        for matrix in range(6):
            owner, offset = where[matrix]
            g = pieces[mine ^ owner][:, offset : offset + PADDED[matrix]].astype(jnp.float32)
            if matrix == DOWN:
                new_down[...] = MOMENTUM * down[...] + g
            elif matrix == EMBED:
                new_embed[...] = MOMENTUM * embed[...] + g[:, :CLASSES]
            else:
                span = slice(OFFSETS[matrix], OFFSETS[matrix] + WIDTHS[matrix])
                new_wide[:, span] = MOMENTUM * wide[:, span] + g

    per_index(bins, index, body)


def update_kernel(bins, index, *rest):
    n = len(bins)
    pieces, (upd_wide, upd_down, upd_embed) = rest[:n], rest[n:]
    where = placed(bins)

    def body(mine):
        for matrix in range(6):
            owner, offset = where[matrix]
            value = pieces[mine ^ owner][:, offset : offset + PADDED[matrix]]
            if matrix == DOWN:
                upd_down[...] = value
            elif matrix == EMBED:
                upd_embed[...] = value[:, :CLASSES]
            else:
                upd_wide[:, OFFSETS[matrix] : OFFSETS[matrix] + WIDTHS[matrix]] = value

    per_index(bins, index, body)


VMEM = pl.BlockSpec(memory_space=pltpu.VMEM)
SMEM = pl.BlockSpec(memory_space=pltpu.SMEM)
ANY = pl.BlockSpec(memory_space=pl.ANY)


def call(kernel, outs, args, specs, scratch=(), flops=0, limit=VMEM_LIMIT):
    size = sum(a.size * a.dtype.itemsize for a in args) + sum(
        math.prod(o.shape) * o.dtype.itemsize for o in outs
    )
    return pl.pallas_call(
        kernel,
        out_shape=tuple(outs),
        in_specs=specs,
        out_specs=tuple([VMEM] * len(outs)),
        scratch_shapes=list(scratch),
        compiler_params=pltpu.CompilerParams(vmem_limit_bytes=limit),
        cost_estimate=pl.CostEstimate(flops=flops, bytes_accessed=size, transcendentals=0),
    )(*args)


def swap(value, axis, k, n):
    return lax.ppermute(value, axis, [(i, i ^ k) for i in range(n)])


def spread(value, axis, n):
    return [swap(value, axis, k, n) for k in range(1, n)]


def stack(pieces, tied=()):
    rows, width = pieces[0].shape
    if rows % 16:
        return jnp.concatenate(pieces, axis=0)
    return call(
        functools.partial(stack_kernel, len(pieces)),
        [jax.ShapeDtypeStruct((rows * len(pieces), width), pieces[0].dtype)],
        (*pieces, *tied),
        [VMEM] * len(pieces) + [ANY] * len(tied),
    )[0]


def per_device(grad_wide, grad_down, grad_embed, mom_wide, mom_down, mom_embed):
    n_rep, n_shard = lax.axis_size("rep"), lax.axis_size("shard")
    bins, width = plan(n_rep)
    index = lax.axis_index("rep").astype(jnp.int32).reshape(1)
    grads = (grad_wide[0, 0], grad_down[0, 0].T, grad_embed[0].T)
    moms = (mom_wide[0], mom_down[0].T, mom_embed.T)
    rows = grads[0].shape[0]
    windows = [(0, width // 2), (width // 2, width)]

    def block(columns, dtype=jnp.bfloat16):
        return jax.ShapeDtypeStruct((rows, columns), dtype)

    sends = call(
        functools.partial(split_kernel, bins, windows),
        [block(high - low) for low, high in windows for _ in range(n_rep)],
        (index, *grads),
        [SMEM] + [ANY] * 3,
        [pltpu.VMEM(array.shape, jnp.float32) for array in grads] + [pltpu.SemaphoreType.DMA((3,))],
        limit=VMEM_ALL,
    )
    mom_own = call(
        functools.partial(own_kernel, bins, windows),
        [block(high - low, jnp.float32) for low, high in windows],
        (index, *moms),
        [SMEM] + [VMEM] * 3,
    )
    gs, arrived = [], []
    for half, (low, high) in enumerate(windows):
        own, *others = sends[half * n_rep : (half + 1) * n_rep]
        received = [own] + [swap(piece, "rep", k + 1, n_rep) for k, piece in enumerate(others)]
        g, y = call(
            functools.partial(sum_kernel, n_rep),
            [block(high - low)] * 2,
            (mom_own[half], *received),
            [VMEM] * (n_rep + 1),
        )
        gs.append(g)
        arrived.append([y] + [swap(y, "shard", k, n_shard) for k in range(2, n_shard, 2)])
    stacks = [None, stack(arrived[1], (arrived[0][0],))]
    (g,) = call(join_kernel, [block(width)], (*gs, arrived[1][1]), [VMEM] * 2 + [ANY])
    g_others = spread(g, "rep", n_rep)
    stacks[0] = stack(arrived[0], g_others[:2])
    pieces = [piece for whole in stacks for piece in (whole, swap(whole, "shard", 1, n_shard))]
    (upd,) = call(
        functools.partial(newton_kernel, bins, 2, 2),
        [block(width)],
        (index, *pieces),
        [SMEM] + [VMEM] * len(pieces),
        (pltpu.VMEM((D, width), jnp.bfloat16),),
        flops=NS_ITERS * (4 * D * D * width + 2 * D * D * D),
    )
    upd_others = spread(upd, "rep", n_rep)
    news = call(
        functools.partial(momentum_kernel, bins),
        [jax.ShapeDtypeStruct(m.shape, jnp.float32) for m in moms],
        (index, *moms, g, *g_others),
        [SMEM] + [VMEM] * (3 + n_rep),
    )
    updates = call(
        functools.partial(update_kernel, bins),
        [jax.ShapeDtypeStruct(m.shape, jnp.bfloat16) for m in moms],
        (index, upd, *upd_others),
        [SMEM] + [VMEM] * n_rep,
    )
    return (
        news[0][None],
        news[1].T[None],
        news[2].T,
        updates[0][None],
        updates[1].T[None],
        updates[2].T,
    )


def solution(mesh):
    placed_in = (
        P("rep", None, "shard", None),
        P("rep", None, None, "shard"),
        P("rep", None, "shard"),
        P(None, "shard", None),
        P(None, None, "shard"),
        P(None, "shard"),
    )
    return jax.shard_map(
        per_device,
        mesh=mesh,
        in_specs=placed_in,
        out_specs=placed_in[3:] + placed_in[3:],
        check_vma=False,
    )
```

```python
import functools
import math

import jax
import jax.numpy as jnp
from jax import lax
from jax.experimental import pallas as pl
from jax.experimental.pallas import tpu as pltpu
from jax.sharding import PartitionSpec as P

D = 384
MLP = 1536
ADA = 2304
CLASSES = 1001
NS_ITERS = 5
QKV = 1152

COEF_A = 3.4445
COEF_B = -4.775
COEF_C = 2.0315
MOMENTUM = 0.95
EPSILON = 1e-07

VMEM_LIMIT = 48 * 1024 * 1024
VMEM_ALL = 62 * 1024 * 1024

WIDTHS = [QKV, D, MLP, ADA, MLP, CLASSES]
OFFSETS = [0, QKV, QKV + D, QKV + D + MLP]
PADDED = [-(-width // 128) * 128 for width in WIDTHS]
DOWN, EMBED = 4, 5
TILE = 256


def plan(n_rep):
    bins = [[] for _ in range(n_rep)]
    loads = [0] * n_rep
    for matrix in sorted(range(6), key=lambda m: -PADDED[m]):
        owner = loads.index(min(loads))
        bins[owner].append(matrix)
        loads[owner] += PADDED[matrix]
    return bins, max(loads)


def window(group, low, high):
    found = []
    offset = 0
    for matrix in group:
        first, last = max(low - offset, 0), min(high - offset, PADDED[matrix])
        if first < last:
            found.append((matrix, first, offset + first - low, last - first))
        offset += PADDED[matrix]
    return found


def columns(matrix, first, width, wide, down, embed):
    if matrix == DOWN:
        return down[:, first : first + width]
    if matrix == EMBED:
        last = min(first + width, CLASSES)
        value = embed[:, first:last]
        if last < first + width:
            tail = jnp.zeros((value.shape[0], first + width - last), value.dtype)
            value = jnp.concatenate([value, tail], axis=1)
        return value
    return wide[:, OFFSETS[matrix] + first : OFFSETS[matrix] + first + width]


def split_kernel(bins, windows, index, wide, down, embed, *rest):
    n = len(bins)
    outs, held, sems = rest[: len(windows) * n], rest[-4:-1], rest[-1]
    copies = [pltpu.make_async_copy(src, dst, sems.at[i]) for i, (src, dst) in enumerate(zip((wide, down, embed), held))]
    for copy in copies:
        copy.start()
    for copy in copies:
        copy.wait()
    for half, (low, high) in enumerate(windows):
        for k in range(n):
            dst = outs[half * n + k]
            for target, group in enumerate(bins):

                @pl.when((index[0] ^ k) == target)
                def _():
                    end = 0
                    for matrix, first, place, width in window(group, low, high):
                        dst[:, place : place + width] = columns(matrix, first, width, *held).astype(dst.dtype)
                        end = place + width
                    if end < high - low:
                        dst[:, end:] = jnp.zeros((dst.shape[0], high - low - end), dst.dtype)


def own_kernel(bins, windows, index, wide, down, embed, *outs):
    for target, group in enumerate(bins):

        @pl.when(index[0] == target)
        def _():
            for out, (low, high) in zip(outs, windows):
                end = 0
                for matrix, first, place, width in window(group, low, high):
                    out[:, place : place + width] = columns(matrix, first, width, wide, down, embed)
                    end = place + width
                if end < high - low:
                    out[:, end:] = jnp.zeros((out.shape[0], high - low - end), out.dtype)


def sum_kernel(count, mom, *rest):
    received, g_out, y_out = rest[:count], rest[-2], rest[-1]
    g = received[0][...].astype(jnp.float32)
    for piece in received[1:]:
        g = g + piece[...].astype(jnp.float32)
    g_out[...] = g.astype(jnp.bfloat16)
    y_out[...] = (g + MOMENTUM * (MOMENTUM * mom[...] + g)).astype(jnp.bfloat16)


def join_kernel(left, right, *rest):
    out, half = rest[-1], left.shape[1]
    out[:, :half] = left[...]
    out[:, half:] = right[...]


def stack_kernel(count, *rest):
    out, rows = rest[-1], rest[0].shape[0]
    for number in range(count):
        out[number * rows : (number + 1) * rows, :] = rest[number][...]


def newton_kernel(bins, halves, count, index, *rest):
    out, x_ref = rest[-2], rest[-1]
    left = 0
    for half in range(halves):
        pieces = rest[half * count : (half + 1) * count]
        top = 0
        for piece in pieces:
            x_ref[top : top + piece.shape[0], left : left + piece.shape[1]] = piece[...]
            top += piece.shape[0]
        left += pieces[0].shape[1]
    rows = out.shape[0]

    def branch(group):
        spans = []
        offset = 0
        for matrix in group:
            end = offset + PADDED[matrix]
            tiles = [slice(low, min(low + TILE, end)) for low in range(offset, end, TILE)]
            spans.append((slice(offset, end), tiles, math.sqrt(max(D, WIDTHS[matrix]))))
            offset = end

        def product(left, right, sides):
            return lax.dot_general(left, right, ((sides[0], sides[1]), ((), ())), preferred_element_type=jnp.float32)

        def grams():
            found = []
            for span, _, _ in spans:
                x = x_ref[:, span]
                found.append(product(x, x, ((1,), (1,))))
            return found

        def polynomials(grams, scales, count=D):
            halves = [gram.astype(jnp.bfloat16) for gram in grams]
            squares = [product(gram[:count], gram, ((1,), (0,))) for gram in halves]
            return [
                (
                    scale
                    * (
                        COEF_B * gram[:count].astype(jnp.float32)
                        + COEF_C * square
                        + jnp.where(diagonal[:count], COEF_A, 0.0)
                    )
                ).astype(jnp.bfloat16)
                for gram, square, scale in zip(halves, squares, scales)
            ]

        def advance(polys):
            for poly, (_, tiles, _) in zip(polys, spans):
                for tile in tiles:
                    x_ref[:, tile] = product(poly, x_ref[:, tile], ((1,), (0,))).astype(jnp.bfloat16)

        row = lax.broadcasted_iota(jnp.int32, (D, D), 0)
        diagonal = row == lax.broadcasted_iota(jnp.int32, (D, D), 1)
        ones = [1.0] * len(spans)
        first = grams()
        scales = [1.0 / (jnp.sqrt(jnp.sum(jnp.where(diagonal, gram, 0.0))) + EPSILON) for gram in first]
        advance(polynomials([gram * scale * scale for gram, scale in zip(first, scales)], scales))

        def step(_, carry):
            advance(polynomials(grams(), ones))
            return carry

        lax.fori_loop(0, NS_ITERS - 2, step, 0)
        for poly, (_, tiles, factor) in zip(polynomials(grams(), ones, rows), spans):
            for tile in tiles:
                value = product(poly, x_ref[:, tile], ((1,), (0,)))
                out[:, tile] = (factor * value).astype(jnp.bfloat16)

    for target, group in enumerate(bins):
        if group:

            @pl.when(index[0] == target)
            def _():
                branch(group)


def placed(bins):
    where = {}
    for owner, group in enumerate(bins):
        offset = 0
        for matrix in group:
            where[matrix] = (owner, offset)
            offset += PADDED[matrix]
    return where


def per_index(bins, index, body):
    for mine in range(len(bins)):

        @pl.when(index[0] == mine)
        def _():
            body(mine)


def momentum_kernel(bins, index, wide, down, embed, *rest):
    n = len(bins)
    pieces, (new_wide, new_down, new_embed) = rest[:n], rest[n:]
    where = placed(bins)

    def body(mine):
        for matrix in range(6):
            owner, offset = where[matrix]
            g = pieces[mine ^ owner][:, offset : offset + PADDED[matrix]].astype(jnp.float32)
            if matrix == DOWN:
                new_down[...] = MOMENTUM * down[...] + g
            elif matrix == EMBED:
                new_embed[...] = MOMENTUM * embed[...] + g[:, :CLASSES]
            else:
                span = slice(OFFSETS[matrix], OFFSETS[matrix] + WIDTHS[matrix])
                new_wide[:, span] = MOMENTUM * wide[:, span] + g

    per_index(bins, index, body)


def update_kernel(bins, index, *rest):
    n = len(bins)
    pieces, (upd_wide, upd_down, upd_embed) = rest[:n], rest[n:]
    where = placed(bins)

    def body(mine):
        for matrix in range(6):
            owner, offset = where[matrix]
            value = pieces[mine ^ owner][:, offset : offset + PADDED[matrix]]
            if matrix == DOWN:
                upd_down[...] = value
            elif matrix == EMBED:
                upd_embed[...] = value[:, :CLASSES]
            else:
                upd_wide[:, OFFSETS[matrix] : OFFSETS[matrix] + WIDTHS[matrix]] = value

    per_index(bins, index, body)


VMEM = pl.BlockSpec(memory_space=pltpu.VMEM)
SMEM = pl.BlockSpec(memory_space=pltpu.SMEM)
ANY = pl.BlockSpec(memory_space=pl.ANY)


def call(kernel, outs, args, specs, scratch=(), flops=0, limit=VMEM_LIMIT):
    size = sum(a.size * a.dtype.itemsize for a in args) + sum(
        math.prod(o.shape) * o.dtype.itemsize for o in outs
    )
    return pl.pallas_call(
        kernel,
        out_shape=tuple(outs),
        in_specs=specs,
        out_specs=tuple([VMEM] * len(outs)),
        scratch_shapes=list(scratch),
        compiler_params=pltpu.CompilerParams(vmem_limit_bytes=limit),
        cost_estimate=pl.CostEstimate(flops=flops, bytes_accessed=size, transcendentals=0),
    )(*args)


def swap(value, axis, k, n):
    return lax.ppermute(value, axis, [(i, i ^ k) for i in range(n)])


def spread(value, axis, n):
    return [swap(value, axis, k, n) for k in range(1, n)]


def stack(pieces, tied=()):
    rows, width = pieces[0].shape
    if rows % 16:
        return jnp.concatenate(pieces, axis=0)
    return call(
        functools.partial(stack_kernel, len(pieces)),
        [jax.ShapeDtypeStruct((rows * len(pieces), width), pieces[0].dtype)],
        (*pieces, *tied),
        [VMEM] * len(pieces) + [ANY] * len(tied),
    )[0]


def per_device(grad_wide, grad_down, grad_embed, mom_wide, mom_down, mom_embed):
    n_rep, n_shard = lax.axis_size("rep"), lax.axis_size("shard")
    bins, width = plan(n_rep)
    index = lax.axis_index("rep").astype(jnp.int32).reshape(1)
    grads = (grad_wide[0, 0], grad_down[0, 0].T, grad_embed[0].T)
    moms = (mom_wide[0], mom_down[0].T, mom_embed.T)
    rows = grads[0].shape[0]
    windows = [(0, width // 2), (width // 2, width)]

    def block(columns, dtype=jnp.bfloat16):
        return jax.ShapeDtypeStruct((rows, columns), dtype)

    sends = call(
        functools.partial(split_kernel, bins, windows),
        [block(high - low) for low, high in windows for _ in range(n_rep)],
        (index, *grads),
        [SMEM] + [ANY] * 3,
        [pltpu.VMEM(array.shape, jnp.float32) for array in grads] + [pltpu.SemaphoreType.DMA((3,))],
        limit=VMEM_ALL,
    )
    mom_own = call(
        functools.partial(own_kernel, bins, windows),
        [block(high - low, jnp.float32) for low, high in windows],
        (index, *moms),
        [SMEM] + [VMEM] * 3,
    )
    gs, arrived = [], []
    for half, (low, high) in enumerate(windows):
        own, *others = sends[half * n_rep : (half + 1) * n_rep]
        received = [own] + [swap(piece, "rep", k + 1, n_rep) for k, piece in enumerate(others)]
        g, y = call(
            functools.partial(sum_kernel, n_rep),
            [block(high - low)] * 2,
            (mom_own[half], *received),
            [VMEM] * (n_rep + 1),
        )
        gs.append(g)
        arrived.append([y] + [swap(y, "shard", k, n_shard) for k in range(2, n_shard, 2)])
    stacks = [None, stack(arrived[1], (arrived[0][0],))]
    (g,) = call(join_kernel, [block(width)], (*gs, arrived[1][1]), [VMEM] * 2 + [ANY])
    g_others = spread(g, "rep", n_rep)
    stacks[0] = stack(arrived[0], g_others[:2])
    pieces = [piece for whole in stacks for piece in (whole, swap(whole, "shard", 1, n_shard))]
    (upd,) = call(
        functools.partial(newton_kernel, bins, 2, 2),
        [block(width)],
        (index, *pieces),
        [SMEM] + [VMEM] * len(pieces),
        (pltpu.VMEM((D, width), jnp.bfloat16),),
        flops=NS_ITERS * (4 * D * D * width + 2 * D * D * D),
    )
    upd_others = spread(upd, "rep", n_rep)
    news = call(
        functools.partial(momentum_kernel, bins),
        [jax.ShapeDtypeStruct(m.shape, jnp.float32) for m in moms],
        (index, *moms, g, *g_others),
        [SMEM] + [VMEM] * (3 + n_rep),
    )
    updates = call(
        functools.partial(update_kernel, bins),
        [jax.ShapeDtypeStruct(m.shape, jnp.bfloat16) for m in moms],
        (index, upd, *upd_others),
        [SMEM] + [VMEM] * n_rep,
    )
    return (
        news[0][None],
        news[1].T[None],
        news[2].T,
        updates[0][None],
        updates[1].T[None],
        updates[2].T,
    )


def solution(mesh):
    placed_in = (
        P("rep", None, "shard", None),
        P("rep", None, None, "shard"),
        P("rep", None, "shard"),
        P(None, "shard", None),
        P(None, None, "shard"),
        P(None, "shard"),
    )
    return jax.shard_map(
        per_device,
        mesh=mesh,
        in_specs=placed_in,
        out_specs=placed_in[3:] + placed_in[3:],
        check_vma=False,
    )
```

```python
import functools
import math

import jax
import jax.numpy as jnp
from jax import lax
from jax.experimental import pallas as pl
from jax.experimental.pallas import tpu as pltpu
from jax.sharding import PartitionSpec as P

D = 384
MLP = 1536
ADA = 2304
CLASSES = 1001
NS_ITERS = 5
QKV = 1152

COEF_A = 3.4445
COEF_B = -4.775
COEF_C = 2.0315
MOMENTUM = 0.95
EPSILON = 1e-07

VMEM_LIMIT = 48 * 1024 * 1024
VMEM_ALL = 62 * 1024 * 1024

WIDTHS = [QKV, D, MLP, ADA, MLP, CLASSES]
OFFSETS = [0, QKV, QKV + D, QKV + D + MLP]
PADDED = [-(-width // 128) * 128 for width in WIDTHS]
DOWN, EMBED = 4, 5
TILE = 768


def plan(n_rep):
    bins = [[] for _ in range(n_rep)]
    loads = [0] * n_rep
    for matrix in sorted(range(6), key=lambda m: -PADDED[m]):
        owner = loads.index(min(loads))
        bins[owner].append(matrix)
        loads[owner] += PADDED[matrix]
    return bins, max(loads)


def window(group, low, high):
    found = []
    offset = 0
    for matrix in group:
        first, last = max(low - offset, 0), min(high - offset, PADDED[matrix])
        if first < last:
            found.append((matrix, first, offset + first - low, last - first))
        offset += PADDED[matrix]
    return found


def columns(matrix, first, width, wide, down, embed):
    if matrix == DOWN:
        return down[:, first : first + width]
    if matrix == EMBED:
        last = min(first + width, CLASSES)
        value = embed[:, first:last]
        if last < first + width:
            tail = jnp.zeros((value.shape[0], first + width - last), value.dtype)
            value = jnp.concatenate([value, tail], axis=1)
        return value
    return wide[:, OFFSETS[matrix] + first : OFFSETS[matrix] + first + width]


def split_kernel(bins, windows, index, wide, down, embed, *rest):
    n = len(bins)
    outs, held, sems = rest[: len(windows) * n], rest[-4:-1], rest[-1]
    copies = []
    for matrix, width in enumerate(WIDTHS):
        src, dst = (down, held[1]) if matrix == DOWN else (embed, held[2]) if matrix == EMBED else (wide, held[0])
        if matrix not in (DOWN, EMBED):
            span = slice(OFFSETS[matrix], OFFSETS[matrix] + width)
            src, dst = src.at[:, span], dst.at[:, span]
        copies.append(pltpu.make_async_copy(src, dst, sems.at[matrix]))
        copies[-1].start()
    for copy in copies:
        copy.wait()
    for half, (low, high) in enumerate(windows):
        for k in range(n):
            dst = outs[half * n + k]
            for target, group in enumerate(bins):

                @pl.when((index[0] ^ k) == target)
                def _():
                    end = 0
                    for matrix, first, place, width in window(group, low, high):
                        dst[:, place : place + width] = columns(matrix, first, width, *held).astype(dst.dtype)
                        end = place + width
                    if end < high - low:
                        dst[:, end:] = jnp.zeros((dst.shape[0], high - low - end), dst.dtype)


def own_kernel(bins, windows, index, wide, down, embed, *outs):
    for target, group in enumerate(bins):

        @pl.when(index[0] == target)
        def _():
            for out, (low, high) in zip(outs, windows):
                end = 0
                for matrix, first, place, width in window(group, low, high):
                    out[:, place : place + width] = columns(matrix, first, width, wide, down, embed)
                    end = place + width
                if end < high - low:
                    out[:, end:] = jnp.zeros((out.shape[0], high - low - end), out.dtype)


def sum_kernel(count, mom, *rest):
    received, g_out, y_out = rest[:count], rest[-2], rest[-1]
    g = received[0][...].astype(jnp.float32)
    for piece in received[1:]:
        g = g + piece[...].astype(jnp.float32)
    g_out[...] = g.astype(jnp.bfloat16)
    y_out[...] = (g + MOMENTUM * (MOMENTUM * mom[...] + g)).astype(jnp.bfloat16)


def join_kernel(left, right, *rest):
    out, half = rest[-1], left.shape[1]
    out[:, :half] = left[...]
    out[:, half:] = right[...]


def stack_kernel(count, *rest):
    out, rows = rest[-1], rest[0].shape[0]
    for number in range(count):
        out[number * rows : (number + 1) * rows, :] = rest[number][...]


def newton_kernel(bins, halves, count, index, *rest):
    out, x_ref = rest[-2], rest[-1]
    left = 0
    for half in range(halves):
        pieces = rest[half * count : (half + 1) * count]
        top = 0
        for piece in pieces:
            x_ref[top : top + piece.shape[0], left : left + piece.shape[1]] = piece[...]
            top += piece.shape[0]
        left += pieces[0].shape[1]
    rows = out.shape[0]

    def branch(group):
        spans = []
        offset = 0
        for matrix in group:
            end = offset + PADDED[matrix]
            tiles = [slice(low, min(low + TILE, end)) for low in range(offset, end, TILE)]
            spans.append((slice(offset, end), tiles, math.sqrt(max(D, WIDTHS[matrix]))))
            offset = end

        def product(left, right, sides):
            return lax.dot_general(left, right, ((sides[0], sides[1]), ((), ())), preferred_element_type=jnp.float32)

        def grams():
            found = []
            for span, _, _ in spans:
                x = x_ref[:, span]
                found.append(product(x, x, ((1,), (1,))))
            return found

        def polynomials(grams, scales, count=D):
            halves = [gram.astype(jnp.bfloat16) for gram in grams]
            squares = [product(gram[:count], gram, ((1,), (0,))) for gram in halves]
            return [
                (
                    scale
                    * (
                        COEF_B * gram[:count].astype(jnp.float32)
                        + COEF_C * square
                        + jnp.where(diagonal[:count], COEF_A, 0.0)
                    )
                ).astype(jnp.bfloat16)
                for gram, square, scale in zip(halves, squares, scales)
            ]

        def advance(polys):
            for poly, (_, tiles, _) in zip(polys, spans):
                for tile in tiles:
                    x_ref[:, tile] = product(poly, x_ref[:, tile], ((1,), (0,))).astype(jnp.bfloat16)

        row = lax.broadcasted_iota(jnp.int32, (D, D), 0)
        diagonal = row == lax.broadcasted_iota(jnp.int32, (D, D), 1)
        ones = [1.0] * len(spans)
        first = grams()
        scales = [1.0 / (jnp.sqrt(jnp.sum(jnp.where(diagonal, gram, 0.0))) + EPSILON) for gram in first]
        advance(polynomials([gram * scale * scale for gram, scale in zip(first, scales)], scales))

        def step(_, carry):
            advance(polynomials(grams(), ones))
            return carry

        lax.fori_loop(0, NS_ITERS - 2, step, 0)
        for poly, (_, tiles, factor) in zip(polynomials(grams(), ones, rows), spans):
            for tile in tiles:
                value = product(poly, x_ref[:, tile], ((1,), (0,)))
                out[:, tile] = (factor * value).astype(jnp.bfloat16)

    for target, group in enumerate(bins):
        if group:

            @pl.when(index[0] == target)
            def _():
                branch(group)


def placed(bins):
    where = {}
    for owner, group in enumerate(bins):
        offset = 0
        for matrix in group:
            where[matrix] = (owner, offset)
            offset += PADDED[matrix]
    return where


def per_index(bins, index, body):
    for mine in range(len(bins)):

        @pl.when(index[0] == mine)
        def _():
            body(mine)


def momentum_kernel(bins, index, wide, down, embed, *rest):
    n = len(bins)
    pieces, (new_wide, new_down, new_embed) = rest[:n], rest[n:]
    where = placed(bins)

    def body(mine):
        for matrix in range(6):
            owner, offset = where[matrix]
            g = pieces[mine ^ owner][:, offset : offset + PADDED[matrix]].astype(jnp.float32)
            if matrix == DOWN:
                new_down[...] = MOMENTUM * down[...] + g
            elif matrix == EMBED:
                new_embed[...] = MOMENTUM * embed[...] + g[:, :CLASSES]
            else:
                span = slice(OFFSETS[matrix], OFFSETS[matrix] + WIDTHS[matrix])
                new_wide[:, span] = MOMENTUM * wide[:, span] + g

    per_index(bins, index, body)


def update_kernel(bins, index, *rest):
    n = len(bins)
    pieces, (upd_wide, upd_down, upd_embed) = rest[:n], rest[n:]
    where = placed(bins)

    def body(mine):
        for matrix in range(6):
            owner, offset = where[matrix]
            value = pieces[mine ^ owner][:, offset : offset + PADDED[matrix]]
            if matrix == DOWN:
                upd_down[...] = value
            elif matrix == EMBED:
                upd_embed[...] = value[:, :CLASSES]
            else:
                upd_wide[:, OFFSETS[matrix] : OFFSETS[matrix] + WIDTHS[matrix]] = value

    per_index(bins, index, body)


VMEM = pl.BlockSpec(memory_space=pltpu.VMEM)
SMEM = pl.BlockSpec(memory_space=pltpu.SMEM)
ANY = pl.BlockSpec(memory_space=pl.ANY)


def call(kernel, outs, args, specs, scratch=(), flops=0, limit=VMEM_LIMIT):
    size = sum(a.size * a.dtype.itemsize for a in args) + sum(
        math.prod(o.shape) * o.dtype.itemsize for o in outs
    )
    return pl.pallas_call(
        kernel,
        out_shape=tuple(outs),
        in_specs=specs,
        out_specs=tuple([VMEM] * len(outs)),
        scratch_shapes=list(scratch),
        compiler_params=pltpu.CompilerParams(vmem_limit_bytes=limit),
        cost_estimate=pl.CostEstimate(flops=flops, bytes_accessed=size, transcendentals=0),
    )(*args)


def swap(value, axis, k, n):
    return lax.ppermute(value, axis, [(i, i ^ k) for i in range(n)])


def spread(value, axis, n):
    return [swap(value, axis, k, n) for k in range(1, n)]


def stack(pieces, tied=()):
    rows, width = pieces[0].shape
    if rows % 16:
        return jnp.concatenate(pieces, axis=0)
    return call(
        functools.partial(stack_kernel, len(pieces)),
        [jax.ShapeDtypeStruct((rows * len(pieces), width), pieces[0].dtype)],
        (*pieces, *tied),
        [VMEM] * len(pieces) + [ANY] * len(tied),
    )[0]


def per_device(grad_wide, grad_down, grad_embed, mom_wide, mom_down, mom_embed):
    n_rep, n_shard = lax.axis_size("rep"), lax.axis_size("shard")
    bins, width = plan(n_rep)
    index = lax.axis_index("rep").astype(jnp.int32).reshape(1)
    grads = (grad_wide[0, 0], grad_down[0, 0].T, grad_embed[0].T)
    moms = (mom_wide[0], mom_down[0].T, mom_embed.T)
    rows = grads[0].shape[0]
    windows = [(0, width // 2), (width // 2, width)]

    def block(columns, dtype=jnp.bfloat16):
        return jax.ShapeDtypeStruct((rows, columns), dtype)

    sends = call(
        functools.partial(split_kernel, bins, windows),
        [block(high - low) for low, high in windows for _ in range(n_rep)],
        (index, *grads),
        [SMEM] + [ANY] * 3,
        [pltpu.VMEM(array.shape, jnp.float32) for array in grads] + [pltpu.SemaphoreType.DMA((6,))],
        limit=VMEM_ALL,
    )
    mom_own = call(
        functools.partial(own_kernel, bins, windows),
        [block(high - low, jnp.float32) for low, high in windows],
        (index, *moms),
        [SMEM] + [VMEM] * 3,
    )
    gs, arrived = [], []
    for half, (low, high) in enumerate(windows):
        own, *others = sends[half * n_rep : (half + 1) * n_rep]
        received = [own] + [swap(piece, "rep", k + 1, n_rep) for k, piece in enumerate(others)]
        g, y = call(
            functools.partial(sum_kernel, n_rep),
            [block(high - low)] * 2,
            (mom_own[half], *received),
            [VMEM] * (n_rep + 1),
        )
        gs.append(g)
        arrived.append([y] + [swap(y, "shard", k, n_shard) for k in range(2, n_shard, 2)])
    stacks = [None, stack(arrived[1], (arrived[0][0],))]
    (g,) = call(join_kernel, [block(width)], (*gs, arrived[1][1]), [VMEM] * 2 + [ANY])
    g_others = spread(g, "rep", n_rep)
    stacks[0] = stack(arrived[0], g_others[:2])
    pieces = [piece for whole in stacks for piece in (whole, swap(whole, "shard", 1, n_shard))]
    (upd,) = call(
        functools.partial(newton_kernel, bins, 2, 2),
        [block(width)],
        (index, *pieces),
        [SMEM] + [VMEM] * len(pieces),
        (pltpu.VMEM((D, width), jnp.bfloat16),),
        flops=NS_ITERS * (4 * D * D * width + 2 * D * D * D),
    )
    upd_others = spread(upd, "rep", n_rep)
    news = call(
        functools.partial(momentum_kernel, bins),
        [jax.ShapeDtypeStruct(m.shape, jnp.float32) for m in moms],
        (index, *moms, g, *g_others),
        [SMEM] + [VMEM] * (3 + n_rep),
    )
    updates = call(
        functools.partial(update_kernel, bins),
        [jax.ShapeDtypeStruct(m.shape, jnp.bfloat16) for m in moms],
        (index, upd, *upd_others),
        [SMEM] + [VMEM] * n_rep,
    )
    return (
        news[0][None],
        news[1].T[None],
        news[2].T,
        updates[0][None],
        updates[1].T[None],
        updates[2].T,
    )


def solution(mesh):
    placed_in = (
        P("rep", None, "shard", None),
        P("rep", None, None, "shard"),
        P("rep", None, "shard"),
        P(None, "shard", None),
        P(None, None, "shard"),
        P(None, "shard"),
    )
    return jax.shard_map(
        per_device,
        mesh=mesh,
        in_specs=placed_in,
        out_specs=placed_in[3:] + placed_in[3:],
        check_vma=False,
    )
```

```python
import functools
import math

import jax
import jax.numpy as jnp
from jax import lax
from jax.experimental import pallas as pl
from jax.experimental.pallas import tpu as pltpu
from jax.sharding import PartitionSpec as P

D = 384
MLP = 1536
ADA = 2304
CLASSES = 1001
NS_ITERS = 5
QKV = 1152

COEF_A = 3.4445
COEF_B = -4.775
COEF_C = 2.0315
MOMENTUM = 0.95
EPSILON = 1e-07

VMEM_LIMIT = 48 * 1024 * 1024
VMEM_ALL = 62 * 1024 * 1024

WIDTHS = [QKV, D, MLP, ADA, MLP, CLASSES]
OFFSETS = [0, QKV, QKV + D, QKV + D + MLP]
PADDED = [-(-width // 128) * 128 for width in WIDTHS]
DOWN, EMBED = 4, 5
TILE = 256


def plan(n_rep):
    bins = [[] for _ in range(n_rep)]
    loads = [0] * n_rep
    for matrix in sorted(range(6), key=lambda m: -PADDED[m]):
        owner = loads.index(min(loads))
        bins[owner].append(matrix)
        loads[owner] += PADDED[matrix]
    order = sorted(range(n_rep), key=lambda owner: loads[owner])
    return [bins[owner] for owner in order], max(loads)


def window(group, low, high):
    found = []
    offset = 0
    for matrix in group:
        first, last = max(low - offset, 0), min(high - offset, PADDED[matrix])
        if first < last:
            found.append((matrix, first, offset + first - low, last - first))
        offset += PADDED[matrix]
    return found


def columns(matrix, first, width, wide, down, embed):
    if matrix == DOWN:
        return down[:, first : first + width]
    if matrix == EMBED:
        last = min(first + width, CLASSES)
        value = embed[:, first:last]
        if last < first + width:
            tail = jnp.zeros((value.shape[0], first + width - last), value.dtype)
            value = jnp.concatenate([value, tail], axis=1)
        return value
    return wide[:, OFFSETS[matrix] + first : OFFSETS[matrix] + first + width]


def split_kernel(bins, windows, index, wide, down, embed, *rest):
    n = len(bins)
    outs, held, sems = rest[: len(windows) * n], rest[-4:-1], rest[-1]
    copies = [pltpu.make_async_copy(src, dst, sems.at[i]) for i, (src, dst) in enumerate(zip((wide, down, embed), held))]
    for copy in copies:
        copy.start()
    for copy in copies:
        copy.wait()
    for half, (low, high) in enumerate(windows):
        for k in range(n):
            dst = outs[half * n + k]
            for target, group in enumerate(bins):

                @pl.when((index[0] ^ k) == target)
                def _():
                    end = 0
                    for matrix, first, place, width in window(group, low, high):
                        dst[:, place : place + width] = columns(matrix, first, width, *held).astype(dst.dtype)
                        end = place + width
                    if end < high - low:
                        dst[:, end:] = jnp.zeros((dst.shape[0], high - low - end), dst.dtype)


def own_kernel(bins, windows, index, wide, down, embed, *outs):
    for target, group in enumerate(bins):

        @pl.when(index[0] == target)
        def _():
            for out, (low, high) in zip(outs, windows):
                end = 0
                for matrix, first, place, width in window(group, low, high):
                    out[:, place : place + width] = columns(matrix, first, width, wide, down, embed)
                    end = place + width
                if end < high - low:
                    out[:, end:] = jnp.zeros((out.shape[0], high - low - end), out.dtype)


def sum_kernel(count, mom, *rest):
    received, g_out, y_out = rest[:count], rest[-2], rest[-1]
    g = received[0][...].astype(jnp.float32)
    for piece in received[1:]:
        g = g + piece[...].astype(jnp.float32)
    g_out[...] = g.astype(jnp.bfloat16)
    y_out[...] = (g + MOMENTUM * (MOMENTUM * mom[...] + g)).astype(jnp.bfloat16)


def join_kernel(left, right, *rest):
    out, half = rest[-1], left.shape[1]
    out[:, :half] = left[...]
    out[:, half:] = right[...]


def stack_kernel(count, *rest):
    out, rows = rest[-1], rest[0].shape[0]
    for number in range(count):
        out[number * rows : (number + 1) * rows, :] = rest[number][...]


def newton_kernel(bins, halves, count, index, *rest):
    out, x_ref = rest[-2], rest[-1]
    left = 0
    for half in range(halves):
        pieces = rest[half * count : (half + 1) * count]
        top = 0
        for piece in pieces:
            x_ref[top : top + piece.shape[0], left : left + piece.shape[1]] = piece[...]
            top += piece.shape[0]
        left += pieces[0].shape[1]
    rows = out.shape[0]

    def branch(group):
        spans = []
        offset = 0
        for matrix in group:
            end = offset + PADDED[matrix]
            tiles = [slice(low, min(low + TILE, end)) for low in range(offset, end, TILE)]
            spans.append((slice(offset, end), tiles, math.sqrt(max(D, WIDTHS[matrix]))))
            offset = end

        def product(left, right, sides):
            return lax.dot_general(left, right, ((sides[0], sides[1]), ((), ())), preferred_element_type=jnp.float32)

        def grams():
            found = []
            for span, _, _ in spans:
                x = x_ref[:, span]
                found.append(product(x, x, ((1,), (1,))))
            return found

        def polynomials(grams, scales, count=D):
            halves = [gram.astype(jnp.bfloat16) for gram in grams]
            squares = [product(gram[:count], gram, ((1,), (0,))) for gram in halves]
            return [
                (
                    scale
                    * (
                        COEF_B * gram[:count].astype(jnp.float32)
                        + COEF_C * square
                        + jnp.where(diagonal[:count], COEF_A, 0.0)
                    )
                ).astype(jnp.bfloat16)
                for gram, square, scale in zip(halves, squares, scales)
            ]

        def advance(polys):
            for poly, (_, tiles, _) in zip(polys, spans):
                for tile in tiles:
                    x_ref[:, tile] = product(poly, x_ref[:, tile], ((1,), (0,))).astype(jnp.bfloat16)

        row = lax.broadcasted_iota(jnp.int32, (D, D), 0)
        diagonal = row == lax.broadcasted_iota(jnp.int32, (D, D), 1)
        ones = [1.0] * len(spans)
        first = grams()
        scales = [1.0 / (jnp.sqrt(jnp.sum(jnp.where(diagonal, gram, 0.0))) + EPSILON) for gram in first]
        advance(polynomials([gram * scale * scale for gram, scale in zip(first, scales)], scales))

        def step(_, carry):
            advance(polynomials(grams(), ones))
            return carry

        lax.fori_loop(0, NS_ITERS - 2, step, 0)
        for poly, (_, tiles, factor) in zip(polynomials(grams(), ones, rows), spans):
            for tile in tiles:
                value = product(poly, x_ref[:, tile], ((1,), (0,)))
                out[:, tile] = (factor * value).astype(jnp.bfloat16)

    for target, group in enumerate(bins):
        if group:

            @pl.when(index[0] == target)
            def _():
                branch(group)


def placed(bins):
    where = {}
    for owner, group in enumerate(bins):
        offset = 0
        for matrix in group:
            where[matrix] = (owner, offset)
            offset += PADDED[matrix]
    return where


def per_index(bins, index, body):
    for mine in range(len(bins)):

        @pl.when(index[0] == mine)
        def _():
            body(mine)


def momentum_kernel(bins, index, wide, down, embed, *rest):
    n = len(bins)
    pieces, (new_wide, new_down, new_embed) = rest[:n], rest[n:]
    where = placed(bins)

    def body(mine):
        for matrix in range(6):
            owner, offset = where[matrix]
            g = pieces[mine ^ owner][:, offset : offset + PADDED[matrix]].astype(jnp.float32)
            if matrix == DOWN:
                new_down[...] = MOMENTUM * down[...] + g
            elif matrix == EMBED:
                new_embed[...] = MOMENTUM * embed[...] + g[:, :CLASSES]
            else:
                span = slice(OFFSETS[matrix], OFFSETS[matrix] + WIDTHS[matrix])
                new_wide[:, span] = MOMENTUM * wide[:, span] + g

    per_index(bins, index, body)


def update_kernel(bins, index, *rest):
    n = len(bins)
    pieces, (upd_wide, upd_down, upd_embed) = rest[:n], rest[n:]
    where = placed(bins)

    def body(mine):
        for matrix in range(6):
            owner, offset = where[matrix]
            value = pieces[mine ^ owner][:, offset : offset + PADDED[matrix]]
            if matrix == DOWN:
                upd_down[...] = value
            elif matrix == EMBED:
                upd_embed[...] = value[:, :CLASSES]
            else:
                upd_wide[:, OFFSETS[matrix] : OFFSETS[matrix] + WIDTHS[matrix]] = value

    per_index(bins, index, body)


VMEM = pl.BlockSpec(memory_space=pltpu.VMEM)
SMEM = pl.BlockSpec(memory_space=pltpu.SMEM)
ANY = pl.BlockSpec(memory_space=pl.ANY)


def call(kernel, outs, args, specs, scratch=(), flops=0, limit=VMEM_LIMIT):
    size = sum(a.size * a.dtype.itemsize for a in args) + sum(
        math.prod(o.shape) * o.dtype.itemsize for o in outs
    )
    return pl.pallas_call(
        kernel,
        out_shape=tuple(outs),
        in_specs=specs,
        out_specs=tuple([VMEM] * len(outs)),
        scratch_shapes=list(scratch),
        compiler_params=pltpu.CompilerParams(vmem_limit_bytes=limit),
        cost_estimate=pl.CostEstimate(flops=flops, bytes_accessed=size, transcendentals=0),
    )(*args)


def swap(value, axis, k, n):
    return lax.ppermute(value, axis, [(i, i ^ k) for i in range(n)])


def spread(value, axis, n):
    return [swap(value, axis, k, n) for k in range(1, n)]


def stack(pieces, tied=()):
    rows, width = pieces[0].shape
    if rows % 16:
        return jnp.concatenate(pieces, axis=0)
    return call(
        functools.partial(stack_kernel, len(pieces)),
        [jax.ShapeDtypeStruct((rows * len(pieces), width), pieces[0].dtype)],
        (*pieces, *tied),
        [VMEM] * len(pieces) + [ANY] * len(tied),
    )[0]


def per_device(grad_wide, grad_down, grad_embed, mom_wide, mom_down, mom_embed):
    n_rep, n_shard = lax.axis_size("rep"), lax.axis_size("shard")
    bins, width = plan(n_rep)
    index = lax.axis_index("rep").astype(jnp.int32).reshape(1)
    grads = (grad_wide[0, 0], grad_down[0, 0].T, grad_embed[0].T)
    moms = (mom_wide[0], mom_down[0].T, mom_embed.T)
    rows = grads[0].shape[0]
    windows = [(0, width // 2), (width // 2, width)]

    def block(columns, dtype=jnp.bfloat16):
        return jax.ShapeDtypeStruct((rows, columns), dtype)

    sends = call(
        functools.partial(split_kernel, bins, windows),
        [block(high - low) for low, high in windows for _ in range(n_rep)],
        (index, *grads),
        [SMEM] + [ANY] * 3,
        [pltpu.VMEM(array.shape, jnp.float32) for array in grads] + [pltpu.SemaphoreType.DMA((3,))],
        limit=VMEM_ALL,
    )
    mom_own = call(
        functools.partial(own_kernel, bins, windows),
        [block(high - low, jnp.float32) for low, high in windows],
        (index, *moms),
        [SMEM] + [VMEM] * 3,
    )
    gs, arrived = [], []
    for half, (low, high) in enumerate(windows):
        own, *others = sends[half * n_rep : (half + 1) * n_rep]
        received = [own] + [swap(piece, "rep", k + 1, n_rep) for k, piece in enumerate(others)]
        g, y = call(
            functools.partial(sum_kernel, n_rep),
            [block(high - low)] * 2,
            (mom_own[half], *received),
            [VMEM] * (n_rep + 1),
        )
        gs.append(g)
        arrived.append([y] + [swap(y, "shard", k, n_shard) for k in range(2, n_shard, 2)])
    stacks = [None, stack(arrived[1], (arrived[0][0],))]
    (g,) = call(join_kernel, [block(width)], (*gs, arrived[1][1]), [VMEM] * 2 + [ANY])
    g_others = spread(g, "rep", n_rep)
    stacks[0] = stack(arrived[0], g_others[:2])
    pieces = [piece for whole in stacks for piece in (whole, swap(whole, "shard", 1, n_shard))]
    (upd,) = call(
        functools.partial(newton_kernel, bins, 2, 2),
        [block(width)],
        (index, *pieces),
        [SMEM] + [VMEM] * len(pieces),
        (pltpu.VMEM((D, width), jnp.bfloat16),),
        flops=NS_ITERS * (4 * D * D * width + 2 * D * D * D),
    )
    upd_others = spread(upd, "rep", n_rep)
    news = call(
        functools.partial(momentum_kernel, bins),
        [jax.ShapeDtypeStruct(m.shape, jnp.float32) for m in moms],
        (index, *moms, g, *g_others),
        [SMEM] + [VMEM] * (3 + n_rep),
    )
    updates = call(
        functools.partial(update_kernel, bins),
        [jax.ShapeDtypeStruct(m.shape, jnp.bfloat16) for m in moms],
        (index, upd, *upd_others),
        [SMEM] + [VMEM] * n_rep,
    )
    return (
        news[0][None],
        news[1].T[None],
        news[2].T,
        updates[0][None],
        updates[1].T[None],
        updates[2].T,
    )


def solution(mesh):
    placed_in = (
        P("rep", None, "shard", None),
        P("rep", None, None, "shard"),
        P("rep", None, "shard"),
        P(None, "shard", None),
        P(None, None, "shard"),
        P(None, "shard"),
    )
    return jax.shard_map(
        per_device,
        mesh=mesh,
        in_specs=placed_in,
        out_specs=placed_in[3:] + placed_in[3:],
        check_vma=False,
    )
```
